256 devices in a mesh: dp: 4 (over y), gx: 4 (over x), gy: 16 (over z, core).
Axes of the slice: x: 4, y: 4, z: 8, core: 2. Of those that a mesh axis runs over, the one named last changes fastest.
Arguments:
- field: bfloat16 [4, 64, 32, 20, 2048], P('dp', 'gx', 'gy'), may hold values from -6 to 6
- cotangent: bfloat16 [4, 64, 32, 20, 2048], P('dp', 'gx', 'gy'), may hold values from -6 to 6
- spectral_weight: bfloat16 [24, 24, 20, 20, 192], P(None, None, None, None, ('gx', 'gy')), may hold values from -2.5 to 2.5
- bypass_weight: bfloat16 [20, 20], replicated, may hold values from -1.25 to 1.25
Outputs:
- grad_field: bfloat16 [4, 64, 32, 20, 2048], P('dp', 'gx', 'gy')
- grad_spectral: float32 [24, 24, 20, 20, 192], P(None, None, None, None, ('gx', 'gy'))
- grad_bypass: float32 [20, 20], replicated
The draws below stay inside these ranges and needn't reach their ends.
All inputs are finite; a program needn't handle non-finite values.
Results may differ from the reference program's by a relative error of at most 0.034.
Values may be sent and summed in bfloat16 or wider, within the bound.
No kernel may reach another device: no remote copies, remote signals or barrier semaphores. Data moves between devices by JAX's collectives and lax.ppermute only.
A program may use at most 192 MiB of HBM per device.

```python
import math
import jax
import jax.numpy as jnp
from jax import lax

C = 20
MX = 12
MY = 12
MZ = 12
MT = 4
NZ = 128
NT = 16
NX = 64
NY = 32
BATCH = 4
KX = 24
KY = 24
KZT = 192


def steps_of(own_key, dims, cuts, smallest, high):
    factor_of = 1.0
    for position, shards_of in cuts:
        steps = jax.random.uniform(jax.random.fold_in(jax.random.fold_in(own_key, 6), position), (shards_of,), jnp.float32, smallest / len(cuts), high / len(cuts))
        factor_of = factor_of * jnp.repeat(jnp.exp(steps), dims[position] // shards_of).reshape((-1,) + (1,) * (len(dims) - 1 - position))
    return factor_of


def gaussian(stream_key, shape, deviation, reach, cuts=(), held_as=jnp.bfloat16):
    level = steps_of(stream_key, shape, cuts, -0.22, 0.18) if cuts else 1.0
    values = jax.random.normal(stream_key, shape, jnp.float32) * deviation * level
    return jnp.minimum(jnp.maximum(values, -reach), reach).astype(held_as)


def setup_inputs(seed: int = 0) -> dict:
    keys = jax.random.split(jax.random.key(seed), 5)
    field = gaussian(keys[0], (BATCH, NX, NY, C, NZ * NT), 1.0, 6.0, ((0, 4), (1, 4), (2, 16)))
    cotangent = gaussian(keys[1], (BATCH, NX, NY, C, NZ * NT), 1.0, 6.0, ((0, 4), (1, 4), (2, 16)))
    spectral_weight = gaussian(keys[2], (KX, KY, C, C, KZT), (C // 4) ** -0.5, 2.5, ((4, 64),))
    bypass_weight = gaussian(keys[3], (C, C), C ** -0.5, 1.25)
    return {"field": field, "cotangent": cotangent, "spectral_weight": spectral_weight, "bypass_weight": bypass_weight}


HIGH = lax.Precision.HIGHEST

def basis(length, kept):
    places = lax.iota(jnp.int32, length)
    orders = lax.iota(jnp.int32, kept)
    cos_arg = places[:, None] * orders[None, :] % length
    sin_arg = places[:, None] * (orders[None, :] + 1) % length
    step_angle = 2.0 * math.pi / length
    scale = math.sqrt(2.0 / length)
    cos_part = jnp.cos(cos_arg.astype(jnp.float32) * step_angle)
    sin_part = jnp.sin(sin_arg.astype(jnp.float32) * step_angle)
    return jnp.concatenate([cos_part, sin_part], axis=1) * scale

def reference(field, cotangent, spectral_weight, bypass_weight):
    table_x = basis(NX, MX)
    table_y = basis(NY, MY)
    table_z = basis(NZ, MZ)
    table_t = basis(NT, MT)
    weight_f = spectral_weight.astype(jnp.float32)
    bypass_f = bypass_weight.astype(jnp.float32)

    def analyze(cells):
        values = cells.astype(jnp.float32).reshape(NX, NY, C, NZ, NT)
        values = jnp.einsum('xycst,tl->xycsl', values, table_t, precision=HIGH)
        values = jnp.einsum('xycsl,sk->xyckl', values, table_z, precision=HIGH)
        coeff = values.reshape(NX, NY, C, KZT).astype(jnp.bfloat16)
        partial_x = jnp.einsum('xycq,xk->kycq', coeff.astype(jnp.float32), table_x, precision=HIGH).astype(jnp.bfloat16)
        return jnp.einsum('kycq,yl->klcq', partial_x.astype(jnp.float32), table_y, precision=HIGH).astype(jnp.bfloat16)

    def synthesize(spectrum):
        partial_y = jnp.einsum('klcq,yl->kycq', spectrum.astype(jnp.float32), table_y, precision=HIGH).astype(jnp.bfloat16)
        partial_x = jnp.einsum('kycq,xk->xycq', partial_y.astype(jnp.float32), table_x, precision=HIGH).astype(jnp.bfloat16)
        values = partial_x.astype(jnp.float32).reshape(NX, NY, C, 2 * MZ, 2 * MT)
        values = jnp.einsum('xyckl,tl->xyckt', values, table_t, precision=HIGH)
        values = jnp.einsum('xyckt,sk->xycst', values, table_z, precision=HIGH)
        return values.reshape(NX, NY, C, NZ * NT)

    def per_sample(sample):
        cells, upstream_in = sample
        spectrum = analyze(cells)
        mixed = jnp.einsum('klcq,klcoq->kloq', spectrum.astype(jnp.float32), weight_f, precision=HIGH).astype(jnp.bfloat16)
        spatial = synthesize(mixed)
        bypass = jnp.einsum('xyip,io->xyop', cells.astype(jnp.float32), bypass_f, precision=HIGH)
        pre = spatial + bypass
        unused, pullback = jax.vjp(jax.nn.gelu, pre)
        slope, = pullback(upstream_in.astype(jnp.float32))
        upstream = slope.astype(jnp.bfloat16)
        bypass_term = jnp.einsum('xyip,xyop->io', cells.astype(jnp.float32), upstream.astype(jnp.float32), precision=HIGH)
        spectrum_up = analyze(upstream)
        spectrum_back = jnp.einsum('kloq,klcoq->klcq', spectrum_up.astype(jnp.float32), weight_f, precision=HIGH).astype(jnp.bfloat16)
        grad_cells = synthesize(spectrum_back) + jnp.einsum('xyop,io->xyip', upstream.astype(jnp.float32), bypass_f, precision=HIGH)
        return (grad_cells.astype(jnp.bfloat16), spectrum, spectrum_up, bypass_term)
    grad_field, spectra, spectra_up, bypass_terms = lax.map(per_sample, (field, cotangent))
    grad_spectral = jnp.einsum('bklcq,bkloq->klcoq', spectra.astype(jnp.float32), spectra_up.astype(jnp.float32), precision=HIGH)
    grad_bypass = lax.optimization_barrier(jnp.sum(bypass_terms, axis=0))
    return (grad_field, grad_spectral, grad_bypass)
```

```python
import math

import jax
import jax.numpy as jnp
import ml_dtypes
import numpy as np
from jax import lax
from jax.experimental import pallas as pl
from jax.experimental.pallas import tpu as pltpu
from jax.sharding import PartitionSpec as P

MX = 12
MY = 12
MZ = 12
MT = 4
NZ = 128
NT = 16
NX = 64
NY = 32
C = 20
KX = 2 * MX
KY = 2 * MY
PX = 4
PY = 16
DEV = PX * PY
CX = NX // PX
CY = NY // PY
NP = NZ * NT
TILES = NP // 128
GROUPS = C // 4
ROWS = C * CX * CY
Q3 = 3
CHUNK = 16
SPEC = Q3 * GROUPS * KY
XB = 4
BLOCK = C * XB * CY
F32 = jnp.float32
BF16 = jnp.bfloat16
MIB = 2**20
VMEM = pl.BlockSpec(memory_space=pltpu.VMEM)
ANY = pl.BlockSpec(memory_space=pl.ANY)


def basis(length, kept):
    places = np.arange(length)[:, None]
    orders = np.arange(kept)[None, :]
    cos_part = np.cos(2 * np.pi * ((places * orders) % length) / length)
    sin_part = np.sin(2 * np.pi * ((places * (orders + 1)) % length) / length)
    return np.concatenate([cos_part, sin_part], axis=1) * math.sqrt(2.0 / length)


def tables():
    fx, fy = basis(NX, MX), basis(NY, MY)
    fzt = (basis(NZ, MZ)[:, None, :, None] * basis(NT, MT)[None, :, None, :]).reshape(NP, -1)
    by_slot = fzt.reshape(NP, DEV, Q3).transpose(0, 2, 1).reshape(NP, Q3 * DEV)
    ahead = np.zeros((NP, 256))
    ahead[:, : Q3 * DEV] = by_slot
    eye4, eye2 = np.eye(4), np.eye(CY)
    slots = np.eye(CHUNK)[:, : Q3 * GROUPS]
    fx32 = np.zeros((NX, 32))
    fx32[:, :KX] = fx
    x_ahead = np.einsum(
        "gxk,cd,yz->gxcyzdk", fx32.reshape(PX, CX, 32), eye4, eye2
    ).reshape(PX * 128, CY * 128)
    y_ahead = np.einsum("gyl,rs->slygr", fy.reshape(PY, CY, KY), slots).reshape(
        SPEC, CY * PY * CHUNK
    )
    spread = np.einsum("cd,kl,e->ckdel", eye4, np.eye(32), np.ones(4)).reshape(128, 512)
    channel = np.einsum("jk,x,cd,y->jxcykd", np.eye(GROUPS), np.ones(XB), eye4, np.ones(CY))
    channel = channel.reshape(BLOCK, C)
    cell = np.einsum("j,xw,c,yz->jxcywz", np.ones(GROUPS), np.eye(XB), np.ones(4), eye2)
    cell = cell.reshape(BLOCK, XB * CY)
    return {
        "zt_ahead": ahead,
        "zt_back": by_slot.T,
        "x_ahead": x_ahead,
        "x_back": x_ahead.T,
        "y_ahead": y_ahead,
        "y_back": y_ahead.T,
        "spread": spread,
        "channel": channel,
        "same": cell @ cell.T,
    }


TABLES = {name: value.astype(ml_dtypes.bfloat16) for name, value in tables().items()}


def dot(a, b, form=((1,), (0,)), precision=None):
    return lax.dot_general(
        a, b, (form, ((), ())), preferred_element_type=F32, precision=precision
    )


def copies(field_ref, rows_ref, sems, back=False):
    made = []
    for tile in range(TILES):
        for j in range(GROUPS):
            outer = field_ref.at[:, pl.ds(4 * j, 4), :, pl.ds(128 * tile, 128)]
            inner = rows_ref.at[tile, j]
            pair = (inner, outer) if back else (outer, inner)
            made.append(pltpu.make_async_copy(*pair, sems.at[tile, j]))
    return made


def pack_chunks(coeff_ref, stage, extra, send_ref):
    for j in range(GROUPS):
        turned = coeff_ref[pl.ds(128 * j, 128), :].T
        for s in range(Q3):
            stage[pl.ds(s * GROUPS + j, DEV, stride=CHUNK), :] = turned[s * DEV : (s + 1) * DEV]
    stage[pl.ds(CHUNK - 1, DEV, stride=CHUNK), :] = extra
    send_ref[...] = stage[...].astype(BF16).reshape(DEV, CHUNK, 128)


def unpack_chunks(recv_ref, stage, coeff_ref):
    stage[...] = recv_ref[...].reshape(DEV * CHUNK, 128).astype(F32)
    for j in range(GROUPS):
        parts = [stage[pl.ds(s * GROUPS + j, DEV, stride=CHUNK), :] for s in range(Q3)]
        coeff_ref[pl.ds(128 * j, 128), :] = jnp.concatenate(parts, axis=0).T.astype(BF16)


def split_three(value):
    high = value.astype(BF16).astype(F32)
    rest = value - high
    middle = rest.astype(BF16).astype(F32)
    low = (rest - middle).astype(BF16).astype(F32)
    return high + pltpu.roll(middle, 32, 1) + pltpu.roll(low, 64, 1)


def join_three(value):
    lanes = lax.broadcasted_iota(jnp.int32, value.shape, 1)
    whole = value + (pltpu.roll(value, 96, 1) + pltpu.roll(value, 64, 1))
    return jnp.where(lanes < 32, whole, 0.0)


def analyze_kernel(field_ref, zt_ref, send_ref, rows_ref, coeff, stage, sems):
    made = copies(field_ref, rows_ref, sems)
    for copy in made:
        copy.start()
    rows = rows_ref.reshape(TILES, ROWS, 128)
    step = 4
    for first in range(0, TILES, step):
        for copy in made[first * GROUPS : (first + step) * GROUPS]:
            copy.wait()
        part = jnp.concatenate([rows[t] for t in range(first, first + step)], axis=1)
        term = dot(part, zt_ref[pl.ds(128 * first, 128 * step), :])
        if first:
            coeff[...] += term
        else:
            coeff[...] = term
    pack_chunks(coeff, stage, jnp.zeros((DEV, 128), F32), send_ref)


def weights_kernel(weight_ref, out_ref):
    gap = jnp.zeros((8, KY), F32)

    def one(o, carry):
        parts = []
        for s in range(Q3):
            for j in range(GROUPS):
                pieces = []
                for c in range(4):
                    pieces += [weight_ref[4 * j + c, o, s].astype(F32), gap]
                parts.append(jnp.concatenate(pieces, axis=0).T)
        out_ref[o] = jnp.concatenate(parts, axis=0).astype(BF16)
        return carry

    lax.fori_loop(0, C, one, 0)


def to_modes(recv_ref, x_ref, y_ref):
    pieces = recv_ref[...].reshape(PX, PY * CHUNK, 128)
    wide = jnp.concatenate([pieces[g] for g in range(PX)], axis=1)
    along = dot(wide, x_ref[...]).astype(BF16)
    tall = jnp.concatenate([along[:, :128], along[:, 128:]], axis=0)
    return dot(y_ref[...], tall).astype(BF16)


def from_modes(modes, y_ref, x_ref):
    tall = dot(y_ref[...], modes.astype(BF16)).astype(BF16)
    half = PY * CHUNK
    wide = jnp.concatenate([tall[:half], tall[half:]], axis=1)
    return dot(wide, x_ref[...])


def write_chunks(values, send_ref):
    for g in range(PX):
        part = values[:, 128 * g : 128 * (g + 1)].astype(BF16)
        send_ref[pl.ds(g * PY, PY)] = part.reshape(PY, CHUNK, 128)


def mix_kernel(
    recv_ref, weight_ref, cot_ref, xa_ref, ya_ref, yb_ref, xb_ref,
    send_ref, spec_ref, rows_ref, modes, sems,
):
    made = copies(cot_ref, rows_ref, sems)
    for copy in made:
        copy.start()
    spec = to_modes(recv_ref, xa_ref, ya_ref)
    spec_ref[...] = spec
    spec = spec.astype(F32)
    group = lax.broadcasted_iota(jnp.int32, (Q3 * KY, 128), 1) // 32
    for jo in range(GROUPS):
        total = jnp.zeros((Q3 * KY, 128), F32)
        for o4 in range(4):
            term = spec * weight_ref[4 * jo + o4].astype(F32)
            sums = []
            for s in range(Q3):
                at = s * GROUPS * KY
                acc = term[at : at + KY]
                for j in range(1, GROUPS):
                    acc = acc + term[at + j * KY : at + (j + 1) * KY]
                sums.append(acc)
            summed = jnp.concatenate(sums, axis=0)
            summed = summed + pltpu.roll(summed, 64, 1)
            summed = summed + pltpu.roll(summed, 32, 1)
            total = jnp.where(group == o4, summed, total)
        for s in range(Q3):
            modes[pl.ds((s * GROUPS + jo) * KY, KY), :] = total[s * KY : (s + 1) * KY]
    write_chunks(from_modes(modes[...], yb_ref, xb_ref), send_ref)
    for copy in made:
        copy.wait()


def mix_back_kernel(
    recv_ref, weight_ref, spread_ref, xa_ref, ya_ref, yb_ref, xb_ref,
    send_ref, spec_ref, stage,
):
    spec = to_modes(recv_ref, xa_ref, ya_ref)
    spec_ref[...] = spec
    copied = dot(spec, spread_ref[...])
    modes = [jnp.zeros((KY, 128), F32) for _ in range(Q3 * GROUPS)]
    for o in range(C):
        weight = weight_ref[o].astype(F32)
        for s in range(Q3):
            at = (s * GROUPS + o // 4) * KY
            source = copied[at : at + KY, 128 * (o % 4) : 128 * (o % 4 + 1)]
            for j in range(GROUPS):
                k = s * GROUPS + j
                modes[k] = modes[k] + weight[k * KY : (k + 1) * KY] * source
    values = from_modes(jnp.concatenate(modes, axis=0), yb_ref, xb_ref)
    stage[...] = recv_ref[...].reshape(DEV * CHUNK, 128).astype(F32)
    extra = stage[pl.ds(CHUNK - 1, DEV, stride=CHUNK), :]
    extra = jnp.broadcast_to(jnp.sum(extra, axis=0, keepdims=True), (8, 128))
    extra = split_three(join_three(extra))[:1]
    row = lax.broadcasted_iota(jnp.int32, values.shape, 0) % CHUNK
    extra = jnp.concatenate([extra] * PX, axis=1)
    write_chunks(jnp.where(row == CHUNK - 1, extra, values), send_ref)


def block_rows(ref, tile, b):
    return [ref[tile, pl.ds(j * 128 + b * 32, 32), :] for j in range(GROUPS)]


def block_of(ref, n, b):
    left = jnp.concatenate(block_rows(ref, 2 * n, b), axis=0)
    right = jnp.concatenate(block_rows(ref, 2 * n + 1, b), axis=0)
    return jnp.concatenate([left, right], axis=1)


def block_store(ref, n, b, value):
    for half in range(2):
        for j in range(GROUPS):
            ref[2 * n + half, pl.ds(j * 128 + b * 32, 32), :] = value[
                32 * j : 32 * (j + 1), 128 * half : 128 * (half + 1)
            ]


def block_rows_of(ref, b):
    return jnp.concatenate([ref[pl.ds(j * 128 + b * 32, 32), :] for j in range(GROUPS)], axis=0)


def bypass_matrix(bypass_ref, channel_ref, same_ref, form):
    half = dot(channel_ref[...], bypass_ref[...], form).astype(BF16)
    whole = dot(half, channel_ref[...], ((1,), (1,)))
    return (whole * same_ref[...].astype(F32)).astype(BF16)


K0 = math.sqrt(2.0 / math.pi)
K1 = 0.044715


def gelu_slope(x):
    square = x * x
    bend = jnp.tanh(x * (K0 + (K0 * K1) * square))
    inner = x * (K0 + (3.0 * K0 * K1) * square)
    return (0.5 + 0.5 * bend) * (1.0 + inner * (1.0 - bend))


def point_kernel(
    recv_ref, field_ref, cot_ref, bypass_ref, channel_ref, same_ref, back_ref, ahead_ref,
    send_ref, up_ref, stage, inverse, coeff, cross, matrix,
):
    unpack_chunks(recv_ref, stage, inverse)
    matrix[...] = bypass_matrix(bypass_ref, channel_ref, same_ref, ((1,), (1,)))
    coeff[...] = jnp.zeros_like(coeff)
    cross[...] = jnp.zeros_like(cross)
    field = field_ref.reshape(TILES, ROWS, 128)
    cot = cot_ref.reshape(TILES, ROWS, 128)

    def part(n, carry):
        lanes = pl.ds(pl.multiple_of(n * 256, 256), 256)
        for b in range(CX // XB):
            cells = block_of(field, n, b)
            pre = dot(block_rows_of(inverse, b), back_ref[:, lanes]) + dot(matrix[...], cells)
            slope = gelu_slope(pre) * block_of(cot, n, b).astype(F32)
            up = slope.astype(BF16)
            block_store(up_ref, n, b, up)
            term = dot(up, ahead_ref[lanes, :])
            for j in range(GROUPS):
                coeff[pl.ds(j * 128 + b * 32, 32), :] += term[32 * j : 32 * (j + 1)]
            cross[...] += dot(cells, up, ((1,), (1,)))
        return carry

    lax.fori_loop(0, TILES // 2, part, 0)
    kept = cross[...] * same_ref[...].astype(F32)
    channel = channel_ref[...].astype(F32)
    high = lax.Precision.HIGHEST
    small = dot(dot(channel, kept, ((0,), (0,)), high), channel, ((1,), (0,)), high)
    small = jnp.concatenate([small, jnp.zeros((C, 128 - C), F32)], axis=1)
    small = jnp.concatenate([small, jnp.zeros((DEV - C, 128), F32)], axis=0)
    pack_chunks(coeff, stage, split_three(small), send_ref)


def final_kernel(
    recv_ref, up_ref, bypass_ref, channel_ref, same_ref, back_ref,
    out_ref, small_ref, stage, inverse, matrix, rows_ref, sems,
):
    unpack_chunks(recv_ref, stage, inverse)
    small_ref[...] = join_three(stage[pl.ds(CHUNK - 1, DEV, stride=CHUNK), :][:24])
    matrix[...] = bypass_matrix(bypass_ref, channel_ref, same_ref, ((1,), (0,)))
    made = copies(out_ref, rows_ref, sems, back=True)
    rows = rows_ref.reshape(TILES, ROWS, 128)
    for n in range(TILES // 2):
        for b in range(CX // XB):
            value = dot(block_rows_of(inverse, b), back_ref[:, 256 * n : 256 * (n + 1)])
            value = value + dot(matrix[...], block_of(up_ref, n, b))
            block_store(rows, n, b, value.astype(BF16))
        for copy in made[2 * n * GROUPS : 2 * (n + 1) * GROUPS]:
            copy.start()
    for copy in made:
        copy.wait()


def outer_kernel(*refs):
    specs, out_ref, first, second = refs[:8], refs[8], refs[9], refs[10]

    @pl.when(pl.program_id(0) == 0)
    def _():
        for b in range(4):
            for ref, tiles in ((specs[b], first), (specs[4 + b], second)):
                value = ref[...].astype(F32)
                for s in range(Q3):
                    for j in range(GROUPS):
                        at = (s * GROUPS + j) * KY
                        turned = value[at : at + KY].T
                        for c in range(4):
                            tiles[4 * j + c, s, b] = turned[32 * c : 32 * c + KX]

    c = pl.program_id(0)
    for s in range(Q3):
        own = [first[c, s, b] for b in range(4)]

        def one(o, carry):
            terms = [own[b] * second[o, s, b] for b in range(4)]
            out_ref[0, o, s] = (terms[0] + terms[2]) + (terms[1] + terms[3])
            return carry

        lax.fori_loop(0, C, one, 0, unroll=4)


def call(kernel, out, in_specs, scratch, **more):
    return pl.pallas_call(
        kernel,
        out_shape=out,
        in_specs=in_specs,
        scratch_shapes=scratch,
        compiler_params=pltpu.CompilerParams(vmem_limit_bytes=40 * MIB),
        **more,
    )


def around(value):
    return [value] + [
        lax.ppermute(value, "dp", [(i, (i + k) % 4) for i in range(4)]) for k in (1, 2, 3)
    ]


def body(field, cotangent, spectral_weight, bypass_weight):
    table = {name: jnp.asarray(value) for name, value in TABLES.items()}
    shape = jax.ShapeDtypeStruct
    chunks = shape((DEV, CHUNK, 128), BF16)
    modes = shape((SPEC, 128), BF16)
    cells = shape((TILES, GROUPS, CX, 4, CY, 128), BF16)
    rows = shape((TILES, ROWS, 128), BF16)
    stage = pltpu.VMEM((DEV * CHUNK, 128), F32)
    sems = pltpu.SemaphoreType.DMA((TILES, GROUPS))
    field_t = jnp.transpose(field[0], (0, 2, 1, 3))
    cot_t = jnp.transpose(cotangent[0], (0, 2, 1, 3))
    weight_t = jnp.transpose(spectral_weight, (2, 3, 4, 0, 1))

    def exchange(value):
        return lax.all_to_all(value, ("gx", "gy"), 0, 0, tiled=True)

    send, field_rows = call(
        analyze_kernel, (chunks, cells), [ANY, VMEM], [pltpu.VMEM((ROWS, 256), F32), stage, sems],
        out_specs=(VMEM, VMEM),
    )(field_t, table["zt_ahead"])
    recv = exchange(send)
    weight = call(
        weights_kernel, shape((C, SPEC, 128), BF16), [VMEM], [], out_specs=VMEM,
    )(weight_t)
    send, spec, cot_rows = call(
        mix_kernel, (chunks, modes, cells), [VMEM, VMEM, ANY] + [VMEM] * 4,
        [pltpu.VMEM((SPEC, 128), F32), sems], out_specs=(VMEM,) * 3,
    )(recv, weight, cot_t, table["x_ahead"], table["y_ahead"], table["y_back"], table["x_back"])
    recv = exchange(send)
    specs = around(spec)
    send, up = call(
        point_kernel, (chunks, rows), [VMEM] * 8,
        [stage, pltpu.VMEM((ROWS, Q3 * DEV), BF16), pltpu.VMEM((ROWS, 256), F32),
         pltpu.VMEM((BLOCK, BLOCK), F32), pltpu.VMEM((BLOCK, BLOCK), BF16)],
        out_specs=(VMEM,) * 2,
    )(recv, field_rows, cot_rows, bypass_weight, table["channel"], table["same"],
      table["zt_back"], table["zt_ahead"])
    recv = exchange(send)
    send, spec_up = call(
        mix_back_kernel, (chunks, modes), [VMEM] * 7, [stage], out_specs=(VMEM,) * 2,
    )(recv, weight, table["spread"], table["x_ahead"], table["y_ahead"], table["y_back"],
      table["x_back"])
    recv = exchange(send)
    specs_up = around(spec_up)
    grad_field, small = call(
        final_kernel, (shape((CX, C, CY, NP), BF16), shape((24, 128), F32)), [VMEM] * 6,
        [stage, pltpu.VMEM((ROWS, Q3 * DEV), BF16), pltpu.VMEM((BLOCK, BLOCK), BF16),
         pltpu.VMEM((TILES, GROUPS, CX, 4, CY, 128), BF16), sems],
        out_specs=(ANY, VMEM),
    )(recv, up, bypass_weight, table["channel"], table["same"], table["zt_back"])
    smalls = around(small)
    grad_bypass = ((smalls[0] + smalls[2]) + (smalls[1] + smalls[3]))[:C, :C]
    grad_spectral = pl.pallas_call(
        outer_kernel,
        grid=(C,),
        out_shape=shape((C, C, Q3, KX, KY), F32),
        in_specs=[pl.BlockSpec((SPEC, 128), lambda c: (0, 0))] * 8,
        out_specs=pl.BlockSpec((1, C, Q3, KX, KY), lambda c: (c, 0, 0, 0, 0)),
        scratch_shapes=[pltpu.VMEM((C, Q3, 4, KX, KY), F32)] * 2,
        compiler_params=pltpu.CompilerParams(vmem_limit_bytes=40 * MIB),
    )(*specs, *specs_up)
    return (
        jnp.transpose(grad_field, (0, 2, 1, 3))[None],
        jnp.transpose(grad_spectral, (3, 4, 0, 1, 2)),
        grad_bypass,
    )


def solution(mesh):
    in_specs = (
        P("dp", "gx", "gy", None, None),
        P("dp", "gx", "gy", None, None),
        P(None, None, None, None, ("gx", "gy")),
        P(),
    )
    out_specs = (P("dp", "gx", "gy", None, None), P(None, None, None, None, ("gx", "gy")), P())
    return jax.shard_map(body, mesh=mesh, in_specs=in_specs, out_specs=out_specs, check_vma=False)
```

```python
import math

import jax
import jax.numpy as jnp
import ml_dtypes
import numpy as np
from jax import lax
from jax.experimental import pallas as pl
from jax.experimental.pallas import tpu as pltpu
from jax.sharding import PartitionSpec as P

MX = 12
MY = 12
MZ = 12
MT = 4
NZ = 128
NT = 16
NX = 64
NY = 32
C = 20
KX = 2 * MX
KY = 2 * MY
PX = 4
PY = 16
DEV = PX * PY
CX = NX // PX
CY = NY // PY
NP = NZ * NT
TILES = NP // 128
GROUPS = C // 4
ROWS = C * CX * CY
Q3 = 3
CHUNK = 16
SPEC = Q3 * GROUPS * KY
XB = 8
PART = 4 * XB * CY
WIDE = 512
STEPS = NP // WIDE
PER = WIDE // 128
NQ = Q3 * DEV
BLOCK = C * XB * CY
F32 = jnp.float32
BF16 = jnp.bfloat16
MIB = 2**20
VMEM = pl.BlockSpec(memory_space=pltpu.VMEM)
HBM = pl.BlockSpec(memory_space=pl.ANY)


def basis(length, kept):
    places = np.arange(length)[:, None]
    orders = np.arange(kept)[None, :]
    cos_part = np.cos(2 * np.pi * ((places * orders) % length) / length)
    sin_part = np.sin(2 * np.pi * ((places * (orders + 1)) % length) / length)
    return np.concatenate([cos_part, sin_part], axis=1) * math.sqrt(2.0 / length)


def tables():
    fx, fy = basis(NX, MX), basis(NY, MY)
    fzt = (basis(NZ, MZ)[:, None, :, None] * basis(NT, MT)[None, :, None, :]).reshape(NP, -1)
    by_slot = fzt.reshape(NP, DEV, Q3).transpose(0, 2, 1).reshape(NP, Q3 * DEV)
    ahead = np.zeros((NP, 256))
    ahead[:, : Q3 * DEV] = by_slot
    eye4, eye2 = np.eye(4), np.eye(CY)
    slots = np.eye(CHUNK)[:, : Q3 * GROUPS]
    fx32 = np.zeros((NX, 32))
    fx32[:, :KX] = fx
    x_ahead = np.einsum(
        "gxk,cd,yz->gxcyzdk", fx32.reshape(PX, CX, 32), eye4, eye2
    ).reshape(PX * 128, CY * 128)
    y_ahead = np.einsum("gyl,rs->slygr", fy.reshape(PY, CY, KY), slots).reshape(
        SPEC, CY * PY * CHUNK
    )
    spread = np.einsum("cd,kl,e->ckdel", eye4, np.eye(32), np.ones(4)).reshape(128, 512)
    channel = np.einsum("jk,x,cd,y->jxcykd", np.eye(GROUPS), np.ones(XB), eye4, np.ones(CY))
    channel = channel.reshape(BLOCK, C)
    cell = np.einsum("j,xw,c,yz->jxcywz", np.ones(GROUPS), np.eye(XB), np.ones(4), eye2)
    cell = cell.reshape(BLOCK, XB * CY)
    return {
        "zt_ahead": ahead,
        "zt_back": by_slot.T,
        "x_ahead": x_ahead,
        "x_back": x_ahead.T,
        "y_ahead": y_ahead,
        "y_back": y_ahead.T,
        "spread": spread,
        "channel": channel,
        "same": np.concatenate([np.zeros((BLOCK, 64)), cell @ cell.T], axis=1),
    }


TABLES = {name: value.astype(ml_dtypes.bfloat16) for name, value in tables().items()}


def dot(a, b, form=((1,), (0,)), precision=None):
    return lax.dot_general(
        a, b, (form, ((), ())), preferred_element_type=F32, precision=precision
    )


def copies(field_ref, rows_ref, sems, back=False):
    made = []
    for tile in range(TILES):
        for j in range(GROUPS):
            outer = field_ref.at[:, pl.ds(4 * j, 4), :, pl.ds(128 * tile, 128)]
            inner = rows_ref.at[tile, j]
            pair = (inner, outer) if back else (outer, inner)
            made.append(pltpu.make_async_copy(*pair, sems.at[tile, j]))
    return made


def pack_chunks(coeff_ref, stage, extra, send_ref):
    for j in range(GROUPS):
        turned = coeff_ref[pl.ds(128 * j, 128), :].T
        for s in range(Q3):
            stage[pl.ds(s * GROUPS + j, DEV, stride=CHUNK), :] = turned[s * DEV : (s + 1) * DEV]
    stage[pl.ds(CHUNK - 1, DEV, stride=CHUNK), :] = extra
    send_ref[...] = stage[...].astype(BF16).reshape(DEV, CHUNK, 128)


def unpack_chunks(recv_ref, stage, left_ref):
    stage[...] = recv_ref[...].reshape(DEV * CHUNK, 128).astype(F32)
    for j in range(GROUPS):
        parts = [stage[pl.ds(s * GROUPS + j, DEV, stride=CHUNK), :] for s in range(Q3)]
        turned = jnp.concatenate(parts, axis=0).T.astype(BF16)
        for b in range(CX // XB):
            left_ref[b, pl.ds(PART * j, PART), pl.ds(0, NQ)] = turned[PART * b : PART * (b + 1)]


def split_three(value):
    high = value.astype(BF16).astype(F32)
    rest = value - high
    middle = rest.astype(BF16).astype(F32)
    low = (rest - middle).astype(BF16).astype(F32)
    return high + pltpu.roll(middle, 32, 1) + pltpu.roll(low, 64, 1)


def join_three(value):
    lanes = lax.broadcasted_iota(jnp.int32, value.shape, 1)
    whole = value + (pltpu.roll(value, 96, 1) + pltpu.roll(value, 64, 1))
    return jnp.where(lanes < 32, whole, 0.0)


def start_all(*pairs):
    made = [pltpu.make_async_copy(*pair) for pair in pairs]
    for copy in made:
        copy.start()
    return made


def analyze_kernel(
    field_ref, zt_hbm, send_ref, rows_hbm, rows_ref, zt_ref, coeff, stage, sems, zt_sems, out_sems,
):
    made = copies(field_ref, rows_ref, sems)
    step = 4
    zt_made = []
    for first in range(0, TILES, step):
        part = pl.ds(128 * first, 128 * step)
        zt_made += start_all((zt_hbm.at[part], zt_ref.at[part], zt_sems.at[first // step]))
        for copy in made[first * GROUPS : (first + step) * GROUPS]:
            copy.start()
    rows = rows_ref.reshape(TILES, ROWS, 128)
    kept = []
    for first in range(0, TILES, step):
        zt_made[first // step].wait()
        for copy in made[first * GROUPS : (first + step) * GROUPS]:
            copy.wait()
        some = pl.ds(first, step)
        kept += start_all((rows_ref.at[some], rows_hbm.at[some], out_sems.at[first // step]))
        part = jnp.concatenate([rows[t] for t in range(first, first + step)], axis=1)
        term = dot(part, zt_ref[pl.ds(128 * first, 128 * step), :])
        if first:
            coeff[...] += term
        else:
            coeff[...] = term
    pack_chunks(coeff, stage, jnp.zeros((DEV, 128), F32), send_ref)
    for copy in kept:
        copy.wait()


def weights_kernel(weight_ref, cot_ref, out_ref, rows_ref, sems):
    made = copies(cot_ref, rows_ref, sems)
    for copy in made:
        copy.start()
    gap = jnp.zeros((8, KY), F32)

    def one(o, carry):
        parts = []
        for s in range(Q3):
            for j in range(GROUPS):
                pieces = []
                for c in range(4):
                    pieces += [weight_ref[4 * j + c, o, s].astype(F32), gap]
                parts.append(jnp.concatenate(pieces, axis=0).T)
        out_ref[o] = jnp.concatenate(parts, axis=0).astype(BF16)
        return carry

    lax.fori_loop(0, C, one, 0)
    for copy in made:
        copy.wait()


def to_modes(recv_ref, x_ref, y_ref):
    pieces = recv_ref[...].reshape(PX, PY * CHUNK, 128)
    wide = jnp.concatenate([pieces[g] for g in range(PX)], axis=1)
    along = dot(wide, x_ref[...]).astype(BF16)
    tall = jnp.concatenate([along[:, :128], along[:, 128:]], axis=0)
    return dot(y_ref[...], tall).astype(BF16)


def from_modes(modes, y_ref, x_ref):
    tall = dot(y_ref[...], modes.astype(BF16)).astype(BF16)
    half = PY * CHUNK
    wide = jnp.concatenate([tall[:half], tall[half:]], axis=1)
    return dot(wide, x_ref[...])


def write_chunks(values, send_ref):
    for g in range(PX):
        part = values[:, 128 * g : 128 * (g + 1)].astype(BF16)
        send_ref[pl.ds(g * PY, PY)] = part.reshape(PY, CHUNK, 128)


def mix_kernel(
    recv_ref, weight_ref, xa_ref, ya_ref, yb_ref, xb_ref, send_ref, spec_ref, modes,
):
    spec = to_modes(recv_ref, xa_ref, ya_ref)
    spec_ref[...] = spec
    spec = spec.astype(F32)
    group = lax.broadcasted_iota(jnp.int32, (Q3 * KY, 128), 1) // 32
    for jo in range(GROUPS):
        total = jnp.zeros((Q3 * KY, 128), F32)
        for o4 in range(4):
            term = spec * weight_ref[4 * jo + o4].astype(F32)
            sums = []
            for s in range(Q3):
                at = s * GROUPS * KY
                acc = term[at : at + KY]
                for j in range(1, GROUPS):
                    acc = acc + term[at + j * KY : at + (j + 1) * KY]
                sums.append(acc)
            summed = jnp.concatenate(sums, axis=0)
            summed = summed + pltpu.roll(summed, 64, 1)
            summed = summed + pltpu.roll(summed, 32, 1)
            total = jnp.where(group == o4, summed, total)
        for s in range(Q3):
            modes[pl.ds((s * GROUPS + jo) * KY, KY), :] = total[s * KY : (s + 1) * KY]
    write_chunks(from_modes(modes[...], yb_ref, xb_ref), send_ref)


def mix_back_kernel(
    recv_ref, weight_ref, spread_ref, xa_ref, ya_ref, yb_ref, xb_ref, send_ref, spec_ref, stage,
):
    spec = to_modes(recv_ref, xa_ref, ya_ref)
    spec_ref[...] = spec
    copied = dot(spec, spread_ref[...])
    modes = [jnp.zeros((KY, 128), F32) for _ in range(Q3 * GROUPS)]
    for o in range(C):
        weight = weight_ref[o].astype(F32)
        for s in range(Q3):
            at = (s * GROUPS + o // 4) * KY
            source = copied[at : at + KY, 128 * (o % 4) : 128 * (o % 4 + 1)]
            for j in range(GROUPS):
                k = s * GROUPS + j
                modes[k] = modes[k] + weight[k * KY : (k + 1) * KY] * source
    values = from_modes(jnp.concatenate(modes, axis=0), yb_ref, xb_ref)
    stage[...] = recv_ref[...].reshape(DEV * CHUNK, 128).astype(F32)
    extra = stage[pl.ds(CHUNK - 1, DEV, stride=CHUNK), :]
    extra = jnp.broadcast_to(jnp.sum(extra, axis=0, keepdims=True), (8, 128))
    extra = split_three(join_three(extra))[:1]
    row = lax.broadcasted_iota(jnp.int32, values.shape, 0) % CHUNK
    extra = jnp.concatenate([extra] * PX, axis=1)
    write_chunks(jnp.where(row == CHUNK - 1, extra, values), send_ref)


def block_of(ref, first, b):
    tiles = []
    for t in range(PER):
        rows = [ref[first + t, pl.ds(j * 128 + b * PART, PART), :] for j in range(GROUPS)]
        tiles.append(jnp.concatenate(rows, axis=0))
    return jnp.concatenate(tiles, axis=1)


def block_store(ref, first, b, value):
    for t in range(PER):
        for j in range(GROUPS):
            ref[first + t, pl.ds(j * 128 + b * PART, PART), :] = value[
                PART * j : PART * (j + 1), 128 * t : 128 * (t + 1)
            ]


def bypass_matrix(bypass_ref, channel_ref, same_ref, form, left_ref):
    half = dot(channel_ref[...], bypass_ref[...], form).astype(BF16)
    shifted = jnp.concatenate([jnp.zeros((64, C), F32), channel_ref[...].astype(F32)], axis=0)
    whole = dot(half, shifted.astype(BF16), ((1,), (1,)))
    whole = (whole * same_ref[...].astype(F32)).astype(BF16)
    for b in range(CX // XB):
        left_ref[b, :, pl.ds(128, BLOCK + 64)] = whole


K0 = math.sqrt(2.0 / math.pi)
K1 = 0.044715


def gelu_slope(x):
    square = x * x
    bend = jnp.tanh(x * (K0 + (K0 * K1) * square))
    inner = x * (K0 + (3.0 * K0 * K1) * square)
    return (0.5 + 0.5 * bend) * (1.0 + inner * (1.0 - bend))


def point_kernel(
    recv_ref, field_hbm, cot_hbm, bypass_ref, channel_ref, same_ref, back_hbm, ahead_hbm,
    send_ref, up_hbm,
    field_ref, cot_ref, back_ref, ahead_ref, up_ref, stage, left, coeff, cross, table_sems, sems,
):
    field_hbm = field_hbm.reshape(TILES, ROWS, 128)
    cot_hbm = cot_hbm.reshape(TILES, ROWS, 128)
    tables_made = start_all((back_hbm, back_ref, table_sems.at[0]))
    made = []
    for n in range(STEPS):
        some = pl.ds(PER * n, PER)
        made.append(
            start_all(
                (field_hbm.at[some], field_ref.at[some], sems.at[0, n]),
                (cot_hbm.at[some], cot_ref.at[some], sems.at[1, n]),
            )
        )
        if n == 0:
            tables_made += start_all((ahead_hbm, ahead_ref, table_sems.at[1]))
    bypass_matrix(bypass_ref, channel_ref, same_ref, ((1,), (1,)), left)
    unpack_chunks(recv_ref, stage, left)
    coeff[...] = jnp.zeros_like(coeff)
    cross[...] = jnp.zeros_like(cross)
    tables_made[0].wait()
    kept = []
    for n in range(STEPS):
        for copy in made[n]:
            copy.wait()
        for b in range(CX // XB):
            cells = block_of(field_ref, PER * n, b)
            right = jnp.concatenate([back_ref[:, WIDE * n : WIDE * (n + 1)], cells], axis=0)
            pre = dot(left[b], right)
            slope = gelu_slope(pre) * block_of(cot_ref, PER * n, b).astype(F32)
            up = slope.astype(BF16)
            block_store(up_ref, PER * n, b, up)
            if n == 0 and b == 0:
                tables_made[1].wait()
            term = dot(up, ahead_ref[WIDE * n : WIDE * (n + 1), :])
            for j in range(GROUPS):
                coeff[pl.ds(j * 128 + b * PART, PART), :] += term[PART * j : PART * (j + 1)]
            cross[...] += dot(cells, up, ((1,), (1,)))
        some = pl.ds(PER * n, PER)
        kept += start_all((up_ref.at[some], up_hbm.at[some], sems.at[2, n]))
    kept_cross = cross[...] * same_ref[:, 64:].astype(F32)
    channel = channel_ref[...].astype(F32)
    high = lax.Precision.HIGHEST
    small = dot(dot(channel, kept_cross, ((0,), (0,)), high), channel, ((1,), (0,)), high)
    small = jnp.concatenate([small, jnp.zeros((C, 128 - C), F32)], axis=1)
    small = jnp.concatenate([small, jnp.zeros((DEV - C, 128), F32)], axis=0)
    pack_chunks(coeff, stage, split_three(small), send_ref)
    for copy in kept:
        copy.wait()


def final_kernel(
    recv_ref, up_hbm, bypass_ref, channel_ref, same_ref, back_hbm,
    out_ref, up_ref, back_ref, stage, left, rows_ref, table_sem, up_sems, sems,
):
    (table_made,) = start_all((back_hbm, back_ref, table_sem))
    up_made = []
    for n in range(STEPS):
        some = pl.ds(PER * n, PER)
        up_made += start_all((up_hbm.at[some], up_ref.at[some], up_sems.at[n]))
    bypass_matrix(bypass_ref, channel_ref, same_ref, ((1,), (0,)), left)
    unpack_chunks(recv_ref, stage, left)
    made = copies(out_ref, rows_ref, sems, back=True)
    rows = rows_ref.reshape(TILES, ROWS, 128)
    table_made.wait()
    for n in range(STEPS):
        up_made[n].wait()
        for b in range(CX // XB):
            cells = block_of(up_ref, PER * n, b)
            right = jnp.concatenate([back_ref[:, WIDE * n : WIDE * (n + 1)], cells], axis=0)
            block_store(rows, PER * n, b, dot(left[b], right).astype(BF16))
        for copy in made[PER * n * GROUPS : PER * (n + 1) * GROUPS]:
            copy.start()
    for copy in made:
        copy.wait()


def turn(ref, b, tiles):
    value = ref[...].astype(F32)
    for s in range(Q3):
        for j in range(GROUPS):
            at = (s * GROUPS + j) * KY
            turned = value[at : at + KY].T
            for c in range(4):
                tiles[4 * j + c, s, b] = turned[32 * c : 32 * c + KX]


PAIR = 4


def outer_kernel(*refs):
    out_ref, first, second = refs[8:]

    @pl.when(pl.program_id(0) == 0)
    def _():
        for b in range(4):
            turn(refs[b], b, first)
            turn(refs[4 + b], b, second)

    c = pl.program_id(0) * PAIR
    for s in range(Q3):
        own = [[first[c + i, s, b] for b in range(4)] for i in range(PAIR)]
        for o in range(C):
            other = [second[o, s, b] for b in range(4)]
            for i in range(PAIR):
                terms = [own[i][b] * other[b] for b in range(4)]
                out_ref[i, o, s] = (terms[0] + terms[2]) + (terms[1] + terms[3])


def small_kernel(recv_ref, small_ref, stage):
    stage[...] = recv_ref[pl.ds(0, 24)].astype(F32)
    small_ref[...] = join_three(stage[:, CHUNK - 1, :])


def call(kernel, out, in_specs, scratch, limit=12, **more):
    return pl.pallas_call(
        kernel,
        out_shape=out,
        in_specs=in_specs,
        scratch_shapes=scratch,
        compiler_params=pltpu.CompilerParams(vmem_limit_bytes=limit * MIB),
        **more,
    )


def around(value):
    return [value] + [
        lax.ppermute(value, "dp", [(i, (i + k) % 4) for i in range(4)]) for k in (1, 2, 3)
    ]


def body(field, cotangent, spectral_weight, bypass_weight):
    table = {name: jnp.asarray(value) for name, value in TABLES.items()}
    shape = jax.ShapeDtypeStruct
    chunks = shape((DEV, CHUNK, 128), BF16)
    modes = shape((SPEC, 128), BF16)
    cells = shape((TILES, GROUPS, CX, 4, CY, 128), BF16)
    rows = shape((TILES, ROWS, 128), BF16)
    stage = pltpu.VMEM((DEV * CHUNK, 128), F32)
    dma = lambda *count: pltpu.SemaphoreType.DMA(count)
    sems = dma(TILES, GROUPS)
    field_t = jnp.transpose(field[0], (0, 2, 1, 3))
    cot_t = jnp.transpose(cotangent[0], (0, 2, 1, 3))
    weight_t = jnp.transpose(spectral_weight, (2, 3, 4, 0, 1))

    def exchange(value):
        return lax.all_to_all(value, ("gx", "gy"), 0, 0, tiled=True)

    send, field_rows = call(
        analyze_kernel, (chunks, cells), [HBM, HBM],
        [pltpu.VMEM(cells.shape, BF16), pltpu.VMEM((NP, 256), BF16),
         pltpu.VMEM((ROWS, 256), F32), stage, sems, dma(4), dma(4)],
        out_specs=(VMEM, HBM), limit=62,
    )(field_t, table["zt_ahead"])
    recv = exchange(send)
    weight, cot_rows = call(
        weights_kernel, (shape((C, SPEC, 128), BF16), cells), [VMEM, HBM], [sems],
        out_specs=(VMEM,) * 2, limit=60,
    )(weight_t, cot_t)
    send, spec = call(
        mix_kernel, (chunks, modes), [VMEM] * 6, [pltpu.VMEM((SPEC, 128), F32)],
        out_specs=(VMEM,) * 2,
    )(recv, weight, table["x_ahead"], table["y_ahead"], table["y_back"], table["x_back"])
    recv = exchange(send)
    specs = around(spec)
    left = pltpu.VMEM((CX // XB, BLOCK, NQ + BLOCK), BF16)
    held = pltpu.VMEM(rows.shape, BF16)
    back = pltpu.VMEM((NQ, NP), BF16)
    recv, *specs = lax.optimization_barrier((recv, *specs))
    send, up = call(
        point_kernel, (chunks, rows), [VMEM, HBM, HBM, VMEM, VMEM, VMEM, HBM, HBM],
        [held, held, back, pltpu.VMEM((NP, 256), BF16), held, stage, left,
         pltpu.VMEM((ROWS, 256), F32), pltpu.VMEM((BLOCK, BLOCK), F32), dma(2), dma(3, STEPS)],
        out_specs=(VMEM, HBM), limit=60,
    )(recv, field_rows, cot_rows, bypass_weight, table["channel"], table["same"],
      table["zt_back"], table["zt_ahead"])
    recv = exchange(send)
    send, spec_up = call(
        mix_back_kernel, (chunks, modes), [VMEM] * 7, [stage], out_specs=(VMEM,) * 2,
    )(recv, weight, table["spread"], table["x_ahead"], table["y_ahead"], table["y_back"],
      table["x_back"])
    recv = exchange(send)
    specs_up = around(spec_up)
    grad_spectral = pl.pallas_call(
        outer_kernel,
        grid=(C // PAIR,),
        out_shape=shape((C, C, Q3, KX, KY), F32),
        in_specs=[VMEM] * 8,
        out_specs=pl.BlockSpec((PAIR, C, Q3, KX, KY), lambda c: (c, 0, 0, 0, 0)),
        scratch_shapes=[pltpu.VMEM((C, Q3, 4, KX, KY), F32)] * 2,
        compiler_params=pltpu.CompilerParams(vmem_limit_bytes=24 * MIB),
        cost_estimate=pl.CostEstimate(
            flops=10**9, bytes_accessed=10**8, transcendentals=0
        ),
    )(*specs, *specs_up)
    recv, grad_spectral = lax.optimization_barrier((recv, grad_spectral))
    small = call(
        small_kernel, shape((24, 128), F32), [VMEM], [pltpu.VMEM((24, CHUNK, 128), F32)],
        out_specs=VMEM,
    )(recv)
    smalls = around(small)
    grad_field = call(
        final_kernel, shape((CX, C, CY, NP), BF16), [VMEM, HBM, VMEM, VMEM, VMEM, HBM],
        [held, back, stage, left, pltpu.VMEM(cells.shape, BF16), pltpu.SemaphoreType.DMA,
         dma(STEPS), sems],
        out_specs=HBM, limit=60,
    )(recv, up, bypass_weight, table["channel"], table["same"], table["zt_back"])
    grad_bypass = ((smalls[0] + smalls[2]) + (smalls[1] + smalls[3]))[:C, :C]
    return (
        jnp.transpose(grad_field, (0, 2, 1, 3))[None],
        jnp.transpose(grad_spectral, (3, 4, 0, 1, 2)),
        grad_bypass,
    )


def solution(mesh):
    in_specs = (
        P("dp", "gx", "gy", None, None),
        P("dp", "gx", "gy", None, None),
        P(None, None, None, None, ("gx", "gy")),
        P(),
    )
    out_specs = (P("dp", "gx", "gy", None, None), P(None, None, None, None, ("gx", "gy")), P())
    return jax.shard_map(body, mesh=mesh, in_specs=in_specs, out_specs=out_specs, check_vma=False)
```

```python
import math

import jax
import jax.numpy as jnp
import ml_dtypes
import numpy as np
from jax import lax
from jax.experimental import pallas as pl
from jax.experimental.pallas import tpu as pltpu
from jax.sharding import PartitionSpec as P

MX = 12
MY = 12
MZ = 12
MT = 4
NZ = 128
NT = 16
NX = 64
NY = 32
C = 20
KX = 2 * MX
KY = 2 * MY
PX = 4
PY = 16
DEV = PX * PY
CX = NX // PX
CY = NY // PY
NP = NZ * NT
TILES = NP // 128
GROUPS = C // 4
ROWS = C * CX * CY
Q3 = 3
CHUNK = 16
SPEC = Q3 * GROUPS * KY
XB = 8
PART = 4 * XB * CY
WIDE = 256
STEPS = NP // WIDE
PER = WIDE // 128
NQ = Q3 * DEV
BLOCK = C * XB * CY
F32 = jnp.float32
BF16 = jnp.bfloat16
MIB = 2**20
VMEM = pl.BlockSpec(memory_space=pltpu.VMEM)
HBM = pl.BlockSpec(memory_space=pl.ANY)


def basis(length, kept):
    places = np.arange(length)[:, None]
    orders = np.arange(kept)[None, :]
    cos_part = np.cos(2 * np.pi * ((places * orders) % length) / length)
    sin_part = np.sin(2 * np.pi * ((places * (orders + 1)) % length) / length)
    return np.concatenate([cos_part, sin_part], axis=1) * math.sqrt(2.0 / length)


def tables():
    fx, fy = basis(NX, MX), basis(NY, MY)
    fzt = (basis(NZ, MZ)[:, None, :, None] * basis(NT, MT)[None, :, None, :]).reshape(NP, -1)
    by_slot = fzt.reshape(NP, DEV, Q3).transpose(0, 2, 1).reshape(NP, Q3 * DEV)
    ahead = np.zeros((NP, 256))
    ahead[:, : Q3 * DEV] = by_slot
    eye4, eye2 = np.eye(4), np.eye(CY)
    slots = np.eye(CHUNK)[:, : Q3 * GROUPS]
    fx32 = np.zeros((NX, 32))
    fx32[:, :KX] = fx
    x_ahead = np.einsum(
        "gxk,cd,yz->gxcyzdk", fx32.reshape(PX, CX, 32), eye4, eye2
    ).reshape(PX * 128, CY * 128)
    y_ahead = np.einsum("gyl,rs->slygr", fy.reshape(PY, CY, KY), slots).reshape(
        SPEC, CY * PY * CHUNK
    )
    spread = np.einsum("cd,kl,e->ckdel", eye4, np.eye(32), np.ones(4)).reshape(128, 512)
    channel = np.einsum("jk,x,cd,y->jxcykd", np.eye(GROUPS), np.ones(XB), eye4, np.ones(CY))
    channel = channel.reshape(BLOCK, C)
    cell = np.einsum("j,xw,c,yz->jxcywz", np.ones(GROUPS), np.eye(XB), np.ones(4), eye2)
    cell = cell.reshape(BLOCK, XB * CY)
    return {
        "zt_ahead": ahead,
        "zt_back": by_slot.T,
        "x_ahead": x_ahead,
        "y_ahead": y_ahead,
        "spread": spread,
        "channel": channel,
        "same": np.concatenate([np.zeros((BLOCK, 64)), cell @ cell.T], axis=1),
    }


TABLES = {name: value.astype(ml_dtypes.bfloat16) for name, value in tables().items()}


def dot(a, b, form=((1,), (0,)), precision=None):
    return lax.dot_general(
        a, b, (form, ((), ())), preferred_element_type=F32, precision=precision
    )


def copies(field_ref, rows_ref, sems, back=False):
    made = []
    for tile in range(TILES):
        for j in range(GROUPS):
            outer = field_ref.at[:, pl.ds(4 * j, 4), :, pl.ds(128 * tile, 128)]
            inner = rows_ref.at[tile, j]
            pair = (inner, outer) if back else (outer, inner)
            made.append(pltpu.make_async_copy(*pair, sems.at[tile, j]))
    return made


def pack_chunks(coeff_ref, stage, extra, send_ref):
    for j in range(GROUPS):
        turned = coeff_ref[pl.ds(128 * j, 128), :].T
        for s in range(Q3):
            stage[pl.ds(s * GROUPS + j, DEV, stride=CHUNK), :] = turned[s * DEV : (s + 1) * DEV]
    stage[pl.ds(CHUNK - 1, DEV, stride=CHUNK), :] = extra
    send_ref[...] = stage[...].astype(BF16).reshape(DEV, CHUNK, 128)


def unpack_chunks(recv_ref, stage, left_ref):
    stage[...] = recv_ref[...].reshape(DEV * CHUNK, 128).astype(F32)
    for j in range(GROUPS):
        parts = [stage[pl.ds(s * GROUPS + j, DEV, stride=CHUNK), :] for s in range(Q3)]
        turned = jnp.concatenate(parts, axis=0).T.astype(BF16)
        for b in range(CX // XB):
            left_ref[b, pl.ds(PART * j, PART), pl.ds(0, NQ)] = turned[PART * b : PART * (b + 1)]


def split_three(value):
    high = value.astype(BF16).astype(F32)
    rest = value - high
    middle = rest.astype(BF16).astype(F32)
    low = (rest - middle).astype(BF16).astype(F32)
    return high + pltpu.roll(middle, 32, 1) + pltpu.roll(low, 64, 1)


def join_three(value):
    lanes = lax.broadcasted_iota(jnp.int32, value.shape, 1)
    whole = value + (pltpu.roll(value, 96, 1) + pltpu.roll(value, 64, 1))
    return jnp.where(lanes < 32, whole, 0.0)


def start_all(*pairs):
    made = [pltpu.make_async_copy(*pair) for pair in pairs]
    for copy in made:
        copy.start()
    return made


def analyze_kernel(
    field_ref, zt_hbm, send_ref, rows_hbm, rows_ref, zt_ref, coeff, stage, sems, zt_sems, out_sems,
):
    made = copies(field_ref, rows_ref, sems)
    step = 2
    zt_made = []
    for first in range(0, TILES, step):
        part = pl.ds(128 * first, 128 * step)
        zt_made += start_all((zt_hbm.at[part], zt_ref.at[part], zt_sems.at[first // step]))
        for copy in made[first * GROUPS : (first + step) * GROUPS]:
            copy.start()
    rows = rows_ref.reshape(TILES, ROWS, 128)
    kept = []
    for first in range(0, TILES, step):
        zt_made[first // step].wait()
        for copy in made[first * GROUPS : (first + step) * GROUPS]:
            copy.wait()
        some = pl.ds(first, step)
        kept += start_all((rows_ref.at[some], rows_hbm.at[some], out_sems.at[first // step]))
        part = jnp.concatenate([rows[t] for t in range(first, first + step)], axis=1)
        term = dot(part, zt_ref[pl.ds(128 * first, 128 * step), :])
        if first:
            coeff[...] += term
        else:
            coeff[...] = term
    pack_chunks(coeff, stage, jnp.zeros((DEV, 128), F32), send_ref)
    for copy in kept:
        copy.wait()


def weights_kernel(weight_ref, cot_ref, out_ref, rows_ref, sems):
    made = copies(cot_ref, rows_ref, sems)
    for copy in made:
        copy.start()
    gap = jnp.zeros((8, KY), F32)

    def one(o, carry):
        parts = []
        for s in range(Q3):
            for j in range(GROUPS):
                pieces = []
                for c in range(4):
                    pieces += [weight_ref[4 * j + c, o, s].astype(F32), gap]
                parts.append(jnp.concatenate(pieces, axis=0).T)
        out_ref[o] = jnp.concatenate(parts, axis=0).astype(BF16)
        return carry

    lax.fori_loop(0, C, one, 0)
    for copy in made:
        copy.wait()


def to_modes(recv_ref, x_ref, y_ref):
    pieces = recv_ref[...].reshape(PX, PY * CHUNK, 128)
    wide = jnp.concatenate([pieces[g] for g in range(PX)], axis=1)
    along = dot(wide, x_ref[...]).astype(BF16)
    tall = jnp.concatenate([along[:, :128], along[:, 128:]], axis=0)
    return dot(y_ref[...], tall).astype(BF16)


def from_modes(modes, y_ref, x_ref):
    tall = dot(y_ref[...], modes.astype(BF16), ((0,), (0,))).astype(BF16)
    half = PY * CHUNK
    wide = jnp.concatenate([tall[:half], tall[half:]], axis=1)
    return dot(wide, x_ref[...], ((1,), (1,)))


def write_chunks(values, send_ref):
    for g in range(PX):
        part = values[:, 128 * g : 128 * (g + 1)].astype(BF16)
        send_ref[pl.ds(g * PY, PY)] = part.reshape(PY, CHUNK, 128)


def mix_kernel(
    recv_ref, weight_ref, xa_ref, ya_ref, send_ref, spec_ref, modes,
):
    spec = to_modes(recv_ref, xa_ref, ya_ref)
    spec_ref[...] = spec
    spec = spec.astype(F32)
    group = lax.broadcasted_iota(jnp.int32, (Q3 * KY, 128), 1) // 32
    for jo in range(GROUPS):
        total = jnp.zeros((Q3 * KY, 128), F32)
        for o4 in range(4):
            term = spec * weight_ref[4 * jo + o4].astype(F32)
            sums = []
            for s in range(Q3):
                at = s * GROUPS * KY
                acc = term[at : at + KY]
                for j in range(1, GROUPS):
                    acc = acc + term[at + j * KY : at + (j + 1) * KY]
                sums.append(acc)
            summed = jnp.concatenate(sums, axis=0)
            summed = summed + pltpu.roll(summed, 64, 1)
            summed = summed + pltpu.roll(summed, 32, 1)
            total = jnp.where(group == o4, summed, total)
        for s in range(Q3):
            modes[pl.ds((s * GROUPS + jo) * KY, KY), :] = total[s * KY : (s + 1) * KY]
    write_chunks(from_modes(modes[...], ya_ref, xa_ref), send_ref)


def mix_back_kernel(
    recv_ref, weight_ref, spread_ref, xa_ref, ya_ref, send_ref, spec_ref, stage,
):
    spec = to_modes(recv_ref, xa_ref, ya_ref)
    spec_ref[...] = spec
    copied = dot(spec, spread_ref[...])
    modes = [jnp.zeros((KY, 128), F32) for _ in range(Q3 * GROUPS)]
    for o in range(C):
        weight = weight_ref[o].astype(F32)
        for s in range(Q3):
            at = (s * GROUPS + o // 4) * KY
            source = copied[at : at + KY, 128 * (o % 4) : 128 * (o % 4 + 1)]
            for j in range(GROUPS):
                k = s * GROUPS + j
                modes[k] = modes[k] + weight[k * KY : (k + 1) * KY] * source
    values = from_modes(jnp.concatenate(modes, axis=0), ya_ref, xa_ref)
    stage[...] = recv_ref[...].reshape(DEV * CHUNK, 128).astype(F32)
    extra = stage[pl.ds(CHUNK - 1, DEV, stride=CHUNK), :]
    extra = jnp.broadcast_to(jnp.sum(extra, axis=0, keepdims=True), (8, 128))
    extra = split_three(join_three(extra))[:1]
    row = lax.broadcasted_iota(jnp.int32, values.shape, 0) % CHUNK
    extra = jnp.concatenate([extra] * PX, axis=1)
    write_chunks(jnp.where(row == CHUNK - 1, extra, values), send_ref)


def block_of(ref, first, b):
    tiles = []
    for t in range(PER):
        rows = [ref[first + t, pl.ds(j * 128 + b * PART, PART), :] for j in range(GROUPS)]
        tiles.append(jnp.concatenate(rows, axis=0))
    return jnp.concatenate(tiles, axis=1)


def block_store(ref, first, b, value):
    for t in range(PER):
        for j in range(GROUPS):
            ref[first + t, pl.ds(j * 128 + b * PART, PART), :] = value[
                PART * j : PART * (j + 1), 128 * t : 128 * (t + 1)
            ]


def bypass_matrix(bypass_ref, channel_ref, same_ref, form, left_ref):
    half = dot(channel_ref[...], bypass_ref[...], form).astype(BF16)
    shifted = jnp.concatenate([jnp.zeros((64, C), F32), channel_ref[...].astype(F32)], axis=0)
    whole = dot(half, shifted.astype(BF16), ((1,), (1,)))
    whole = (whole * same_ref[...].astype(F32)).astype(BF16)
    for b in range(CX // XB):
        left_ref[b, :, pl.ds(128, BLOCK + 64)] = whole


K0 = math.sqrt(2.0 / math.pi)
K1 = 0.044715


def gelu_slope(x):
    square = x * x
    bend = jnp.tanh(x * (K0 + (K0 * K1) * square))
    inner = x * (K0 + (3.0 * K0 * K1) * square)
    return (0.5 + 0.5 * bend) * (1.0 + inner * (1.0 - bend))


def point_kernel(
    recv_ref, field_hbm, cot_hbm, bypass_ref, channel_ref, same_ref, back_hbm, ahead_hbm,
    send_ref, up_hbm,
    field_ref, cot_ref, back_ref, ahead_ref, up_ref, stage, left, coeff, cross, table_sems, sems,
):
    field_hbm = field_hbm.reshape(TILES, ROWS, 128)
    cot_hbm = cot_hbm.reshape(TILES, ROWS, 128)
    made = []
    for n in range(STEPS):
        some, lanes = pl.ds(PER * n, PER), pl.ds(WIDE * n, WIDE)
        made.append(
            start_all(
                (back_hbm.at[:, lanes], back_ref.at[:, lanes], table_sems.at[0, n]),
                (field_hbm.at[some], field_ref.at[some], sems.at[0, n]),
                (cot_hbm.at[some], cot_ref.at[some], sems.at[1, n]),
                (ahead_hbm.at[lanes], ahead_ref.at[lanes], table_sems.at[1, n]),
            )
        )
    bypass_matrix(bypass_ref, channel_ref, same_ref, ((1,), (1,)), left)
    unpack_chunks(recv_ref, stage, left)
    coeff[...] = jnp.zeros_like(coeff)
    cross[...] = jnp.zeros_like(cross)
    kept = []
    for n in range(STEPS):
        for copy in made[n]:
            copy.wait()
        for b in range(CX // XB):
            cells = block_of(field_ref, PER * n, b)
            right = jnp.concatenate([back_ref[:, WIDE * n : WIDE * (n + 1)], cells], axis=0)
            pre = dot(left[b], right)
            slope = gelu_slope(pre) * block_of(cot_ref, PER * n, b).astype(F32)
            up = slope.astype(BF16)
            block_store(up_ref, PER * n, b, up)
            term = dot(up, ahead_ref[WIDE * n : WIDE * (n + 1), :])
            for j in range(GROUPS):
                coeff[pl.ds(j * 128 + b * PART, PART), :] += term[PART * j : PART * (j + 1)]
            cross[...] += dot(cells, up, ((1,), (1,)))
        some = pl.ds(PER * n, PER)
        kept += start_all((up_ref.at[some], up_hbm.at[some], sems.at[2, n]))
    kept_cross = cross[...] * same_ref[:, 64:].astype(F32)
    channel = channel_ref[...].astype(F32)
    high = lax.Precision.HIGHEST
    small = dot(dot(channel, kept_cross, ((0,), (0,)), high), channel, ((1,), (0,)), high)
    small = jnp.concatenate([small, jnp.zeros((C, 128 - C), F32)], axis=1)
    small = jnp.concatenate([small, jnp.zeros((DEV - C, 128), F32)], axis=0)
    pack_chunks(coeff, stage, split_three(small), send_ref)
    for copy in kept:
        copy.wait()


def final_kernel(
    recv_ref, up_hbm, bypass_ref, channel_ref, same_ref, back_hbm,
    out_ref, up_ref, back_ref, stage, left, rows_ref, table_sems, up_sems, sems,
):
    loads = []
    for n in range(STEPS):
        some, lanes = pl.ds(PER * n, PER), pl.ds(WIDE * n, WIDE)
        loads.append(
            start_all(
                (back_hbm.at[:, lanes], back_ref.at[:, lanes], table_sems.at[n]),
                (up_hbm.at[some], up_ref.at[some], up_sems.at[n]),
            )
        )
    bypass_matrix(bypass_ref, channel_ref, same_ref, ((1,), (0,)), left)
    unpack_chunks(recv_ref, stage, left)
    made = copies(out_ref, rows_ref, sems, back=True)
    rows = rows_ref.reshape(TILES, ROWS, 128)
    for n in range(STEPS):
        for copy in loads[n]:
            copy.wait()
        for b in range(CX // XB):
            cells = block_of(up_ref, PER * n, b)
            right = jnp.concatenate([back_ref[:, WIDE * n : WIDE * (n + 1)], cells], axis=0)
            block_store(rows, PER * n, b, dot(left[b], right).astype(BF16))
        for copy in made[PER * n * GROUPS : PER * (n + 1) * GROUPS]:
            copy.start()
    for copy in made:
        copy.wait()


def turn(ref, b, tiles):
    value = ref[...].astype(F32)
    for s in range(Q3):
        for j in range(GROUPS):
            at = (s * GROUPS + j) * KY
            turned = value[at : at + KY].T
            for c in range(4):
                tiles[4 * j + c, s, b] = turned[32 * c : 32 * c + KX]


PAIR = 4


def outer_kernel(*refs):
    out_ref, first, second = refs[8:]

    @pl.when(pl.program_id(0) == 0)
    def _():
        for b in range(4):
            turn(refs[b], b, first)
            turn(refs[4 + b], b, second)

    c = pl.program_id(0) * PAIR
    for s in range(Q3):
        own = [[first[c + i, s, b] for b in range(4)] for i in range(PAIR)]
        for o in range(C):
            other = [second[o, s, b] for b in range(4)]
            for i in range(PAIR):
                terms = [own[i][b] * other[b] for b in range(4)]
                out_ref[i, o, s] = (terms[0] + terms[2]) + (terms[1] + terms[3])


def small_kernel(recv_ref, small_ref, stage):
    stage[...] = recv_ref[pl.ds(0, 24)].astype(F32)
    small_ref[...] = join_three(stage[:, CHUNK - 1, :])


def call(kernel, out, in_specs, scratch, limit=12, **more):
    return pl.pallas_call(
        kernel,
        out_shape=out,
        in_specs=in_specs,
        scratch_shapes=scratch,
        compiler_params=pltpu.CompilerParams(vmem_limit_bytes=limit * MIB),
        **more,
    )


def around(value):
    return [value] + [
        lax.ppermute(value, "dp", [(i, (i + k) % 4) for i in range(4)]) for k in (1, 2, 3)
    ]


def body(field, cotangent, spectral_weight, bypass_weight):
    table = {name: jnp.asarray(value) for name, value in TABLES.items()}
    shape = jax.ShapeDtypeStruct
    chunks = shape((DEV, CHUNK, 128), BF16)
    modes = shape((SPEC, 128), BF16)
    cells = shape((TILES, GROUPS, CX, 4, CY, 128), BF16)
    rows = shape((TILES, ROWS, 128), BF16)
    stage = pltpu.VMEM((DEV * CHUNK, 128), F32)
    dma = lambda *count: pltpu.SemaphoreType.DMA(count)
    sems = dma(TILES, GROUPS)
    field_t = jnp.transpose(field[0], (0, 2, 1, 3))
    cot_t = jnp.transpose(cotangent[0], (0, 2, 1, 3))
    weight_t = jnp.transpose(spectral_weight, (2, 3, 4, 0, 1))

    def exchange(value):
        return lax.all_to_all(value, ("gx", "gy"), 0, 0, tiled=True)

    send, field_rows = call(
        analyze_kernel, (chunks, cells), [HBM, HBM],
        [pltpu.VMEM(cells.shape, BF16), pltpu.VMEM((NP, 256), BF16),
         pltpu.VMEM((ROWS, 256), F32), stage, sems, dma(8), dma(8)],
        out_specs=(VMEM, HBM), limit=62,
    )(field_t, table["zt_ahead"])
    recv = exchange(send)
    weight, cot_rows = call(
        weights_kernel, (shape((C, SPEC, 128), BF16), cells), [VMEM, HBM], [sems],
        out_specs=(VMEM,) * 2, limit=60,
    )(weight_t, cot_t)
    send, spec = call(
        mix_kernel, (chunks, modes), [VMEM] * 4, [pltpu.VMEM((SPEC, 128), F32)],
        out_specs=(VMEM,) * 2,
    )(recv, weight, table["x_ahead"], table["y_ahead"])
    recv = exchange(send)
    specs = around(spec)
    left = pltpu.VMEM((CX // XB, BLOCK, NQ + BLOCK), BF16)
    held = pltpu.VMEM(rows.shape, BF16)
    back = pltpu.VMEM((NQ, NP), BF16)
    recv, *specs = lax.optimization_barrier((recv, *specs))
    send, up = call(
        point_kernel, (chunks, rows), [VMEM, HBM, HBM, VMEM, VMEM, VMEM, HBM, HBM],
        [held, held, back, pltpu.VMEM((NP, 256), BF16), held, stage, left,
         pltpu.VMEM((ROWS, 256), F32), pltpu.VMEM((BLOCK, BLOCK), F32), dma(2, STEPS), dma(3, STEPS)],
        out_specs=(VMEM, HBM), limit=60,
    )(recv, field_rows, cot_rows, bypass_weight, table["channel"], table["same"],
      table["zt_back"], table["zt_ahead"])
    recv = exchange(send)
    send, spec_up = call(
        mix_back_kernel, (chunks, modes), [VMEM] * 5, [stage], out_specs=(VMEM,) * 2,
    )(recv, weight, table["spread"], table["x_ahead"], table["y_ahead"])
    recv = exchange(send)
    specs_up = around(spec_up)
    grad_spectral = pl.pallas_call(
        outer_kernel,
        grid=(C // PAIR,),
        out_shape=shape((C, C, Q3, KX, KY), F32),
        in_specs=[VMEM] * 8,
        out_specs=pl.BlockSpec((PAIR, C, Q3, KX, KY), lambda c: (c, 0, 0, 0, 0)),
        scratch_shapes=[pltpu.VMEM((C, Q3, 4, KX, KY), F32)] * 2,
        compiler_params=pltpu.CompilerParams(vmem_limit_bytes=24 * MIB),
        cost_estimate=pl.CostEstimate(
            flops=10**9, bytes_accessed=10**8, transcendentals=0
        ),
    )(*specs, *specs_up)
    recv, grad_spectral = lax.optimization_barrier((recv, grad_spectral))
    small = call(
        small_kernel, shape((24, 128), F32), [VMEM], [pltpu.VMEM((24, CHUNK, 128), F32)],
        out_specs=VMEM,
    )(recv)
    smalls = around(small)
    grad_field = call(
        final_kernel, shape((CX, C, CY, NP), BF16), [VMEM, HBM, VMEM, VMEM, VMEM, HBM],
        [held, back, stage, left, pltpu.VMEM(cells.shape, BF16), dma(STEPS),
         dma(STEPS), sems],
        out_specs=HBM, limit=60,
    )(recv, up, bypass_weight, table["channel"], table["same"], table["zt_back"])
    grad_bypass = ((smalls[0] + smalls[2]) + (smalls[1] + smalls[3]))[:C, :C]
    return (
        jnp.transpose(grad_field, (0, 2, 1, 3))[None],
        jnp.transpose(grad_spectral, (3, 4, 0, 1, 2)),
        grad_bypass,
    )


def solution(mesh):
    in_specs = (
        P("dp", "gx", "gy", None, None),
        P("dp", "gx", "gy", None, None),
        P(None, None, None, None, ("gx", "gy")),
        P(),
    )
    out_specs = (P("dp", "gx", "gy", None, None), P(None, None, None, None, ("gx", "gy")), P())
    return jax.shard_map(body, mesh=mesh, in_specs=in_specs, out_specs=out_specs, check_vma=False)
```

```python
import math

import jax
import jax.numpy as jnp
import ml_dtypes
import numpy as np
from jax import lax
from jax.experimental import pallas as pl
from jax.experimental.pallas import tpu as pltpu
from jax.sharding import PartitionSpec as P

MX = 12
MY = 12
MZ = 12
MT = 4
NZ = 128
NT = 16
NX = 64
NY = 32
C = 20
KX = 2 * MX
KY = 2 * MY
PX = 4
PY = 16
DEV = PX * PY
CX = NX // PX
CY = NY // PY
NP = NZ * NT
TILES = NP // 128
GROUPS = C // 4
ROWS = C * CX * CY
Q3 = 3
CHUNK = 16
SPEC = Q3 * GROUPS * KY
PACK = (SPEC + KY) // 4
XB = 8
PART = 4 * XB * CY
WIDE = 512
STEPS = NP // WIDE
PER = WIDE // 128
NQ = Q3 * DEV
BLOCK = C * XB * CY
F32 = jnp.float32
BF16 = jnp.bfloat16
MIB = 2**20
VMEM = pl.BlockSpec(memory_space=pltpu.VMEM)
HBM = pl.BlockSpec(memory_space=pl.ANY)


def basis(length, kept):
    places = np.arange(length)[:, None]
    orders = np.arange(kept)[None, :]
    cos_part = np.cos(2 * np.pi * ((places * orders) % length) / length)
    sin_part = np.sin(2 * np.pi * ((places * (orders + 1)) % length) / length)
    return np.concatenate([cos_part, sin_part], axis=1) * math.sqrt(2.0 / length)


def tables():
    fx, fy = basis(NX, MX), basis(NY, MY)
    fzt = (basis(NZ, MZ)[:, None, :, None] * basis(NT, MT)[None, :, None, :]).reshape(NP, -1)
    by_slot = fzt.reshape(NP, DEV, Q3).transpose(0, 2, 1).reshape(NP, Q3 * DEV)
    ahead = np.zeros((NP, 256))
    ahead[:, : Q3 * DEV] = by_slot
    eye4, eye2 = np.eye(4), np.eye(CY)
    slots = np.eye(CHUNK)[:, : Q3 * GROUPS]
    fx32 = np.zeros((NX, 32))
    fx32[:, :KX] = fx
    x_ahead = np.einsum(
        "gxk,cd,yz->gxcyzdk", fx32.reshape(PX, CX, 32), eye4, eye2
    ).reshape(PX * 128, CY * 128)
    y_ahead = np.einsum("gyl,rs->slygr", fy.reshape(PY, CY, KY), slots).reshape(
        SPEC, CY * PY * CHUNK
    )
    spread = np.einsum("cd,kl,e->ckdel", eye4, np.eye(32), np.ones(4)).reshape(128, 512)
    channel = np.einsum("jk,x,cd,y->jxcykd", np.eye(GROUPS), np.ones(XB), eye4, np.ones(CY))
    channel = channel.reshape(BLOCK, C)
    cell = np.einsum("j,xw,c,yz->jxcywz", np.ones(GROUPS), np.eye(XB), np.ones(4), eye2)
    cell = cell.reshape(BLOCK, XB * CY)
    return {
        "zt_ahead": ahead,
        "zt_back": by_slot.T,
        "x_ahead": x_ahead,
        "y_ahead": y_ahead,
        "spread": spread,
        "channel": channel,
        "same": np.concatenate([np.zeros((BLOCK, 64)), cell @ cell.T], axis=1),
    }


TABLES = {name: value.astype(ml_dtypes.bfloat16) for name, value in tables().items()}


def dot(a, b, form=((1,), (0,)), precision=None):
    return lax.dot_general(
        a, b, (form, ((), ())), preferred_element_type=F32, precision=precision
    )


def copies(field_ref, rows_ref, sems, back=False):
    made = []
    for tile in range(TILES):
        for j in range(GROUPS):
            outer = field_ref.at[:, pl.ds(4 * j, 4), :, pl.ds(128 * tile, 128)]
            inner = rows_ref.at[tile, j]
            pair = (inner, outer) if back else (outer, inner)
            made.append(pltpu.make_async_copy(*pair, sems.at[tile, j]))
    return made


def pack_chunks(coeff_ref, stage, extra, send_ref):
    for j in range(GROUPS):
        turned = coeff_ref[pl.ds(128 * j, 128), :].T
        for s in range(Q3):
            stage[pl.ds(s * GROUPS + j, DEV, stride=CHUNK), :] = turned[s * DEV : (s + 1) * DEV]
    stage[pl.ds(CHUNK - 1, DEV, stride=CHUNK), :] = extra
    send_ref[...] = stage[...].astype(BF16).reshape(DEV, CHUNK, 128)


def unpack_chunks(recv_ref, stage, left_ref):
    stage[...] = recv_ref[...].reshape(DEV * CHUNK, 128).astype(F32)
    for j in range(GROUPS):
        parts = [stage[pl.ds(s * GROUPS + j, DEV, stride=CHUNK), :] for s in range(Q3)]
        turned = jnp.concatenate(parts, axis=0).T.astype(BF16)
        for b in range(CX // XB):
            left_ref[b, pl.ds(PART * j, PART), pl.ds(0, NQ)] = turned[PART * b : PART * (b + 1)]


def split_three(value):
    high = value.astype(BF16).astype(F32)
    rest = value - high
    middle = rest.astype(BF16).astype(F32)
    low = (rest - middle).astype(BF16).astype(F32)
    return high + pltpu.roll(middle, 32, 1) + pltpu.roll(low, 64, 1)


def join_three(value):
    lanes = lax.broadcasted_iota(jnp.int32, value.shape, 1)
    whole = value + (pltpu.roll(value, 96, 1) + pltpu.roll(value, 64, 1))
    return jnp.where(lanes < 32, whole, 0.0)


def start_all(*pairs):
    made = [pltpu.make_async_copy(*pair) for pair in pairs]
    for copy in made:
        copy.start()
    return made


def analyze_kernel(
    field_ref, zt_hbm, send_ref, rows_hbm, rows_ref, zt_ref, coeff, stage, sems, zt_sems, out_sems,
):
    made = copies(field_ref, rows_ref, sems)
    step = 4
    zt_made = []
    for first in range(0, TILES, step):
        part = pl.ds(128 * first, 128 * step)
        zt_made += start_all((zt_hbm.at[part], zt_ref.at[part], zt_sems.at[first // step]))
        for copy in made[first * GROUPS : (first + step) * GROUPS]:
            copy.start()
    rows = rows_ref.reshape(TILES, ROWS, 128)
    kept = []
    for first in range(0, TILES, step):
        zt_made[first // step].wait()
        for copy in made[first * GROUPS : (first + step) * GROUPS]:
            copy.wait()
        some = pl.ds(first, step)
        kept += start_all((rows_ref.at[some], rows_hbm.at[some], out_sems.at[first // step]))
        part = jnp.concatenate([rows[t] for t in range(first, first + step)], axis=1)
        term = dot(part, zt_ref[pl.ds(128 * first, 128 * step), :])
        if first:
            coeff[...] += term
        else:
            coeff[...] = term
    pack_chunks(coeff, stage, jnp.zeros((DEV, 128), F32), send_ref)
    for copy in kept:
        copy.wait()


def weights_kernel(weight_ref, cot_ref, out_ref, rows_ref, sems):
    made = copies(cot_ref, rows_ref, sems)
    for copy in made:
        copy.start()
    gap = jnp.zeros((8, KY), F32)

    def one(o, carry):
        parts = []
        for s in range(Q3):
            for j in range(GROUPS):
                pieces = []
                for c in range(4):
                    pieces += [weight_ref[4 * j + c, o, s].astype(F32), gap]
                parts.append(jnp.concatenate(pieces, axis=0).T)
        out_ref[o] = jnp.concatenate(parts, axis=0).astype(BF16)
        return carry

    lax.fori_loop(0, C, one, 0)
    for copy in made:
        copy.wait()


def to_modes(recv_ref, x_ref, y_ref):
    pieces = recv_ref[...].reshape(PX, PY * CHUNK, 128)
    wide = jnp.concatenate([pieces[g] for g in range(PX)], axis=1)
    along = dot(wide, x_ref[...]).astype(BF16)
    tall = jnp.concatenate([along[:, :128], along[:, 128:]], axis=0)
    return dot(y_ref[...], tall).astype(BF16)


def from_modes(modes, y_ref, x_ref):
    tall = dot(y_ref[...], modes.astype(BF16), ((0,), (0,))).astype(BF16)
    half = PY * CHUNK
    wide = jnp.concatenate([tall[:half], tall[half:]], axis=1)
    return dot(wide, x_ref[...], ((1,), (1,)))


def pack_modes(spec):
    full = jnp.concatenate([spec, jnp.zeros((KY, 128), F32)], axis=0)
    last = full[3 * PACK :]
    inside = lax.broadcasted_iota(jnp.int32, (PACK, 128), 1) % 32 < KX
    parts = []
    for i in range(3):
        moved = pltpu.roll(last, KX - 8 * i, 1)
        parts.append(jnp.where(inside, full[PACK * i : PACK * (i + 1)], moved))
    return jnp.concatenate(parts, axis=0).astype(BF16)


def unpack_modes(packed):
    lane = lax.broadcasted_iota(jnp.int32, (PACK, 128), 1) % 32
    last = jnp.zeros((PACK, 128), F32)
    for i in range(3):
        part = packed[PACK * i : PACK * (i + 1)]
        moved = pltpu.roll(part, 128 - KX + 8 * i, 1)
        last = jnp.where((lane >= 8 * i) & (lane < 8 * (i + 1)), moved, last)
    return jnp.concatenate([packed, last], axis=0)


def write_chunks(values, send_ref):
    for g in range(PX):
        part = values[:, 128 * g : 128 * (g + 1)].astype(BF16)
        send_ref[pl.ds(g * PY, PY)] = part.reshape(PY, CHUNK, 128)


def mix_kernel(
    recv_ref, weight_ref, xa_ref, ya_ref, send_ref, spec_ref, modes,
):
    spec = to_modes(recv_ref, xa_ref, ya_ref).astype(F32)
    spec_ref[...] = pack_modes(spec)
    group = lax.broadcasted_iota(jnp.int32, (Q3 * KY, 128), 1) // 32
    for jo in range(GROUPS):
        total = jnp.zeros((Q3 * KY, 128), F32)
        for o4 in range(4):
            term = spec * weight_ref[4 * jo + o4].astype(F32)
            sums = []
            for s in range(Q3):
                at = s * GROUPS * KY
                acc = term[at : at + KY]
                for j in range(1, GROUPS):
                    acc = acc + term[at + j * KY : at + (j + 1) * KY]
                sums.append(acc)
            summed = jnp.concatenate(sums, axis=0)
            summed = summed + pltpu.roll(summed, 64, 1)
            summed = summed + pltpu.roll(summed, 32, 1)
            total = jnp.where(group == o4, summed, total)
        for s in range(Q3):
            modes[pl.ds((s * GROUPS + jo) * KY, KY), :] = total[s * KY : (s + 1) * KY]
    write_chunks(from_modes(modes[...], ya_ref, xa_ref), send_ref)


def mix_back_kernel(
    recv_ref, weight_ref, spread_ref, xa_ref, ya_ref, own_ref, send_ref, spec_ref, stage,
):
    spec = to_modes(recv_ref, xa_ref, ya_ref)
    spec_ref[pl.ds(0, 3 * PACK), :] = own_ref[...]
    spec_ref[pl.ds(3 * PACK, 3 * PACK), :] = pack_modes(spec.astype(F32))
    copied = dot(spec, spread_ref[...])
    modes = [jnp.zeros((KY, 128), F32) for _ in range(Q3 * GROUPS)]
    for o in range(C):
        weight = weight_ref[o].astype(F32)
        for s in range(Q3):
            at = (s * GROUPS + o // 4) * KY
            source = copied[at : at + KY, 128 * (o % 4) : 128 * (o % 4 + 1)]
            for j in range(GROUPS):
                k = s * GROUPS + j
                modes[k] = modes[k] + weight[k * KY : (k + 1) * KY] * source
    values = from_modes(jnp.concatenate(modes, axis=0), ya_ref, xa_ref)
    stage[...] = recv_ref[...].reshape(DEV * CHUNK, 128).astype(F32)
    extra = stage[pl.ds(CHUNK - 1, DEV, stride=CHUNK), :]
    extra = jnp.broadcast_to(jnp.sum(extra, axis=0, keepdims=True), (8, 128))
    extra = split_three(join_three(extra))[:1]
    row = lax.broadcasted_iota(jnp.int32, values.shape, 0) % CHUNK
    extra = jnp.concatenate([extra] * PX, axis=1)
    write_chunks(jnp.where(row == CHUNK - 1, extra, values), send_ref)


def block_of(ref, first, b):
    tiles = []
    for t in range(PER):
        rows = [ref[first + t, pl.ds(j * 128 + b * PART, PART), :] for j in range(GROUPS)]
        tiles.append(jnp.concatenate(rows, axis=0))
    return jnp.concatenate(tiles, axis=1)


def block_store(ref, first, b, value):
    for t in range(PER):
        for j in range(GROUPS):
            ref[first + t, pl.ds(j * 128 + b * PART, PART), :] = value[
                PART * j : PART * (j + 1), 128 * t : 128 * (t + 1)
            ]


def bypass_matrix(bypass_ref, channel_ref, same_ref, form, left_ref):
    half = dot(channel_ref[...], bypass_ref[...], form).astype(BF16)
    shifted = jnp.concatenate([jnp.zeros((64, C), F32), channel_ref[...].astype(F32)], axis=0)
    whole = dot(half, shifted.astype(BF16), ((1,), (1,)))
    whole = (whole * same_ref[...].astype(F32)).astype(BF16)
    for b in range(CX // XB):
        left_ref[b, :, pl.ds(128, BLOCK + 64)] = whole


K0 = math.sqrt(2.0 / math.pi)
K1 = 0.044715


def gelu_slope(x):
    square = x * x
    bend = jnp.tanh(x * (K0 + (K0 * K1) * square))
    inner = x * (K0 + (3.0 * K0 * K1) * square)
    return (0.5 + 0.5 * bend) * (1.0 + inner * (1.0 - bend))


def point_kernel(
    recv_ref, field_hbm, cot_hbm, bypass_ref, channel_ref, same_ref, back_ref, ahead_ref,
    send_ref, up_hbm, field_ref, cot_ref, up_ref, stage, left, coeff, cross, sems,
):
    field_hbm = field_hbm.reshape(TILES, ROWS, 128)
    cot_hbm = cot_hbm.reshape(TILES, ROWS, 128)
    made = []
    for n in range(STEPS):
        some = pl.ds(PER * n, PER)
        made.append(
            start_all(
                (field_hbm.at[some], field_ref.at[some], sems.at[1, n]),
                (cot_hbm.at[some], cot_ref.at[some], sems.at[2, n]),
            )
        )
    bypass_matrix(bypass_ref, channel_ref, same_ref, ((1,), (1,)), left)
    unpack_chunks(recv_ref, stage, left)
    coeff[...] = jnp.zeros_like(coeff)
    cross[...] = jnp.zeros_like(cross)
    kept = []
    for n in range(STEPS):
        for copy in made[n]:
            copy.wait()
        for b in range(CX // XB):
            cells = block_of(field_ref, PER * n, b)
            right = jnp.concatenate([back_ref[:, WIDE * n : WIDE * (n + 1)], cells], axis=0)
            pre = dot(left[b], right)
            slope = gelu_slope(pre) * block_of(cot_ref, PER * n, b).astype(F32)
            up = slope.astype(BF16)
            block_store(up_ref, PER * n, b, up)
            term = dot(up, ahead_ref[WIDE * n : WIDE * (n + 1), :])
            for j in range(GROUPS):
                coeff[pl.ds(j * 128 + b * PART, PART), :] += term[PART * j : PART * (j + 1)]
            cross[...] += dot(cells, up, ((1,), (1,)))
        some = pl.ds(PER * n, PER)
        kept += start_all((up_ref.at[some], up_hbm.at[some], sems.at[0, n]))
    kept_cross = cross[...] * same_ref[:, 64:].astype(F32)
    channel = channel_ref[...].astype(F32)
    high = lax.Precision.HIGHEST
    small = dot(dot(channel, kept_cross, ((0,), (0,)), high), channel, ((1,), (0,)), high)
    small = jnp.concatenate([small, jnp.zeros((C, 128 - C), F32)], axis=1)
    small = jnp.concatenate([small, jnp.zeros((DEV - C, 128), F32)], axis=0)
    pack_chunks(coeff, stage, split_three(small), send_ref)
    for copy in kept:
        copy.wait()


def final_kernel(
    recv_ref, up_hbm, bypass_ref, channel_ref, same_ref, back_hbm,
    out_ref, up_ref, back_ref, stage, left, rows_ref, table_sem, up_sems, sems,
):
    (table_made,) = start_all((back_hbm, back_ref, table_sem))
    up_made = []
    for n in range(STEPS):
        some = pl.ds(PER * n, PER)
        up_made += start_all((up_hbm.at[some], up_ref.at[some], up_sems.at[n]))
    bypass_matrix(bypass_ref, channel_ref, same_ref, ((1,), (0,)), left)
    unpack_chunks(recv_ref, stage, left)
    made = copies(out_ref, rows_ref, sems, back=True)
    rows = rows_ref.reshape(TILES, ROWS, 128)
    table_made.wait()
    for n in range(STEPS):
        up_made[n].wait()
        for b in range(CX // XB):
            cells = block_of(up_ref, PER * n, b)
            right = jnp.concatenate([back_ref[:, WIDE * n : WIDE * (n + 1)], cells], axis=0)
            block_store(rows, PER * n, b, dot(left[b], right).astype(BF16))
        for copy in made[PER * n * GROUPS : PER * (n + 1) * GROUPS]:
            copy.start()
    for copy in made:
        copy.wait()


def turn(value, b, tiles):
    for s in range(Q3):
        for j in range(GROUPS):
            at = (s * GROUPS + j) * KY
            turned = value[at : at + KY].T
            for c in range(4):
                tiles[4 * j + c, s, b] = turned[32 * c : 32 * c + KX]


PAIR = 4


def outer_kernel(*refs):
    out_ref, first, second = refs[4:]

    @pl.when(pl.program_id(0) == 0)
    def _():
        for b in range(4):
            both = refs[b][...].astype(F32)
            turn(unpack_modes(both[: 3 * PACK]), b, first)
            turn(unpack_modes(both[3 * PACK :]), b, second)

    c = pl.program_id(0) * PAIR
    for s in range(Q3):
        own = [[first[c + i, s, b] for b in range(4)] for i in range(PAIR)]
        for o in range(C):
            other = [second[o, s, b] for b in range(4)]
            for i in range(PAIR):
                terms = [own[i][b] * other[b] for b in range(4)]
                out_ref[i, o, s] = (terms[0] + terms[2]) + (terms[1] + terms[3])


def small_kernel(recv_ref, small_ref, stage):
    stage[...] = recv_ref[pl.ds(0, 24)].astype(F32)
    small_ref[...] = join_three(stage[:, CHUNK - 1, :])


def call(kernel, out, in_specs, scratch, limit=12, **more):
    return pl.pallas_call(
        kernel,
        out_shape=out,
        in_specs=in_specs,
        scratch_shapes=scratch,
        compiler_params=pltpu.CompilerParams(vmem_limit_bytes=limit * MIB),
        **more,
    )


def around(value):
    return [value] + [
        lax.ppermute(value, "dp", [(i, (i + k) % 4) for i in range(4)]) for k in (1, 2, 3)
    ]


def body(field, cotangent, spectral_weight, bypass_weight):
    table = {name: jnp.asarray(value) for name, value in TABLES.items()}
    shape = jax.ShapeDtypeStruct
    chunks = shape((DEV, CHUNK, 128), BF16)
    cells = shape((TILES, GROUPS, CX, 4, CY, 128), BF16)
    rows = shape((TILES, ROWS, 128), BF16)
    stage = pltpu.VMEM((DEV * CHUNK, 128), F32)
    dma = lambda *count: pltpu.SemaphoreType.DMA(count)
    sems = dma(TILES, GROUPS)
    field_t = jnp.transpose(field[0], (0, 2, 1, 3))
    cot_t = jnp.transpose(cotangent[0], (0, 2, 1, 3))
    weight_t = jnp.transpose(spectral_weight, (2, 3, 4, 0, 1))

    def exchange(value):
        return lax.all_to_all(value, ("gx", "gy"), 0, 0, tiled=True)

    send, field_rows = call(
        analyze_kernel, (chunks, cells), [HBM, HBM],
        [pltpu.VMEM(cells.shape, BF16), pltpu.VMEM((NP, 256), BF16),
         pltpu.VMEM((ROWS, 256), F32), stage, sems, dma(4), dma(4)],
        out_specs=(VMEM, HBM), limit=62,
    )(field_t, table["zt_ahead"])
    recv = exchange(send)
    weight, cot_rows = call(
        weights_kernel, (shape((C, SPEC, 128), BF16), cells), [VMEM, HBM], [sems],
        out_specs=(VMEM,) * 2, limit=60,
    )(weight_t, cot_t)
    send, own = call(
        mix_kernel, (chunks, shape((3 * PACK, 128), BF16)), [VMEM] * 4,
        [pltpu.VMEM((SPEC, 128), F32)], out_specs=(VMEM,) * 2, limit=12,
    )(recv, weight, table["x_ahead"], table["y_ahead"])
    recv = exchange(send)
    left = pltpu.VMEM((CX // XB, BLOCK, NQ + BLOCK), BF16)
    held = pltpu.VMEM(rows.shape, BF16)
    back = pltpu.VMEM((NQ, NP), BF16)
    send, up = call(
        point_kernel, (chunks, rows), [VMEM, HBM, HBM] + [VMEM] * 5,
        [held, held, held, stage, left, pltpu.VMEM((ROWS, 256), F32),
         pltpu.VMEM((BLOCK, BLOCK), F32), dma(3, STEPS)],
        out_specs=(VMEM, HBM), limit=51,
    )(recv, field_rows, cot_rows, bypass_weight, table["channel"], table["same"],
      table["zt_back"], table["zt_ahead"])
    recv = exchange(send)
    send, both = call(
        mix_back_kernel, (chunks, shape((6 * PACK, 128), BF16)), [VMEM] * 6, [stage],
        out_specs=(VMEM,) * 2,
    )(recv, weight, table["spread"], table["x_ahead"], table["y_ahead"], own)
    recv = exchange(send)
    specs = around(both)
    grad_spectral = pl.pallas_call(
        outer_kernel,
        grid=(C // PAIR,),
        out_shape=shape((C, C, Q3, KX, KY), F32),
        in_specs=[VMEM] * 4,
        out_specs=pl.BlockSpec((PAIR, C, Q3, KX, KY), lambda c: (c, 0, 0, 0, 0)),
        scratch_shapes=[pltpu.VMEM((C, Q3, 4, KX, KY), F32)] * 2,
        compiler_params=pltpu.CompilerParams(vmem_limit_bytes=24 * MIB),
        cost_estimate=pl.CostEstimate(
            flops=10**9, bytes_accessed=10**8, transcendentals=0
        ),
    )(*specs)
    recv, grad_spectral = lax.optimization_barrier((recv, grad_spectral))
    small = call(
        small_kernel, shape((24, 128), F32), [VMEM], [pltpu.VMEM((24, CHUNK, 128), F32)],
        out_specs=VMEM,
    )(recv)
    smalls = around(small)
    grad_field = call(
        final_kernel, shape((CX, C, CY, NP), BF16), [VMEM, HBM, VMEM, VMEM, VMEM, HBM],
        [held, back, stage, left, pltpu.VMEM(cells.shape, BF16), pltpu.SemaphoreType.DMA,
         dma(STEPS), sems],
        out_specs=HBM, limit=60,
    )(recv, up, bypass_weight, table["channel"], table["same"], table["zt_back"])
    grad_bypass = ((smalls[0] + smalls[2]) + (smalls[1] + smalls[3]))[:C, :C]
    return (
        jnp.transpose(grad_field, (0, 2, 1, 3))[None],
        jnp.transpose(grad_spectral, (3, 4, 0, 1, 2)),
        grad_bypass,
    )


def solution(mesh):
    in_specs = (
        P("dp", "gx", "gy", None, None),
        P("dp", "gx", "gy", None, None),
        P(None, None, None, None, ("gx", "gy")),
        P(),
    )
    out_specs = (P("dp", "gx", "gy", None, None), P(None, None, None, None, ("gx", "gy")), P())
    return jax.shard_map(body, mesh=mesh, in_specs=in_specs, out_specs=out_specs, check_vma=False)
```

```python
import math

import jax
import jax.numpy as jnp
import ml_dtypes
import numpy as np
from jax import lax
from jax.experimental import pallas as pl
from jax.experimental.pallas import tpu as pltpu
from jax.sharding import PartitionSpec as P

MX = 12
MY = 12
MZ = 12
MT = 4
NZ = 128
NT = 16
NX = 64
NY = 32
C = 20
KX = 2 * MX
KY = 2 * MY
PX = 4
PY = 16
DEV = PX * PY
CX = NX // PX
CY = NY // PY
NP = NZ * NT
TILES = NP // 128
GROUPS = C // 4
ROWS = C * CX * CY
Q3 = 3
CHUNK = 16
SPEC = Q3 * GROUPS * KY
PACK = (SPEC + KY) // 4
XB = 8
PART = 4 * XB * CY
WIDE = 512
STEPS = NP // WIDE
PER = WIDE // 128
NQ = Q3 * DEV
BLOCK = C * XB * CY
F32 = jnp.float32
BF16 = jnp.bfloat16
MIB = 2**20
VMEM = pl.BlockSpec(memory_space=pltpu.VMEM)
HBM = pl.BlockSpec(memory_space=pl.ANY)


def basis(length, kept):
    places = np.arange(length)[:, None]
    orders = np.arange(kept)[None, :]
    cos_part = np.cos(2 * np.pi * ((places * orders) % length) / length)
    sin_part = np.sin(2 * np.pi * ((places * (orders + 1)) % length) / length)
    return np.concatenate([cos_part, sin_part], axis=1) * math.sqrt(2.0 / length)


def tables():
    fx, fy = basis(NX, MX), basis(NY, MY)
    fzt = (basis(NZ, MZ)[:, None, :, None] * basis(NT, MT)[None, :, None, :]).reshape(NP, -1)
    by_slot = fzt.reshape(NP, DEV, Q3).transpose(0, 2, 1).reshape(NP, Q3 * DEV)
    ahead = np.zeros((NP, 256))
    ahead[:, : Q3 * DEV] = by_slot
    eye4, eye2 = np.eye(4), np.eye(CY)
    slots = np.eye(CHUNK)[:, : Q3 * GROUPS]
    fx32 = np.zeros((NX, 32))
    fx32[:, :KX] = fx
    x_ahead = np.einsum(
        "gxk,cd,yz->gxcyzdk", fx32.reshape(PX, CX, 32), eye4, eye2
    ).reshape(PX * 128, CY * 128)
    y_ahead = np.einsum("gyl,rs->slygr", fy.reshape(PY, CY, KY), slots).reshape(
        SPEC, CY * PY * CHUNK
    )
    channel = np.einsum("jk,x,cd,y->jxcykd", np.eye(GROUPS), np.ones(XB), eye4, np.ones(CY))
    channel = channel.reshape(BLOCK, C)
    cell = np.einsum("j,xw,c,yz->jxcywz", np.ones(GROUPS), np.eye(XB), np.ones(4), eye2)
    cell = cell.reshape(BLOCK, XB * CY)
    return {
        "zt_ahead": ahead,
        "zt_back": by_slot.T,
        "x_ahead": x_ahead,
        "y_ahead": y_ahead,
        "channel": channel,
        "same": np.concatenate([np.zeros((BLOCK, 64)), cell @ cell.T], axis=1),
    }


TABLES = {name: value.astype(ml_dtypes.bfloat16) for name, value in tables().items()}


def dot(a, b, form=((1,), (0,)), precision=None):
    return lax.dot_general(
        a, b, (form, ((), ())), preferred_element_type=F32, precision=precision
    )


def copies(field_ref, rows_ref, sems, back=False):
    made = []
    for tile in range(TILES):
        for j in range(GROUPS):
            outer = field_ref.at[:, pl.ds(4 * j, 4), :, pl.ds(128 * tile, 128)]
            inner = rows_ref.at[tile, j]
            pair = (inner, outer) if back else (outer, inner)
            made.append(pltpu.make_async_copy(*pair, sems.at[tile, j]))
    return made


def pack_chunks(coeff_ref, stage, extra, send_ref):
    for j in range(GROUPS):
        turned = coeff_ref[pl.ds(128 * j, 128), :].T
        for s in range(Q3):
            stage[pl.ds(s * GROUPS + j, DEV, stride=CHUNK), :] = turned[s * DEV : (s + 1) * DEV]
    stage[pl.ds(CHUNK - 1, DEV, stride=CHUNK), :] = extra
    send_ref[...] = stage[...].astype(BF16).reshape(DEV, CHUNK, 128)


def unpack_chunks(recv_ref, stage, left_ref):
    stage[...] = recv_ref[...].reshape(DEV * CHUNK, 128).astype(F32)
    for j in range(GROUPS):
        parts = [stage[pl.ds(s * GROUPS + j, DEV, stride=CHUNK), :] for s in range(Q3)]
        turned = jnp.concatenate(parts, axis=0).T.astype(BF16)
        for b in range(CX // XB):
            left_ref[b, pl.ds(PART * j, PART), pl.ds(0, NQ)] = turned[PART * b : PART * (b + 1)]


def split_three(value):
    high = value.astype(BF16).astype(F32)
    rest = value - high
    middle = rest.astype(BF16).astype(F32)
    low = (rest - middle).astype(BF16).astype(F32)
    return high + pltpu.roll(middle, 32, 1) + pltpu.roll(low, 64, 1)


def join_three(value):
    lanes = lax.broadcasted_iota(jnp.int32, value.shape, 1)
    whole = value + (pltpu.roll(value, 96, 1) + pltpu.roll(value, 64, 1))
    return jnp.where(lanes < 32, whole, 0.0)


def start_all(*pairs):
    made = [pltpu.make_async_copy(*pair) for pair in pairs]
    for copy in made:
        copy.start()
    return made


def analyze_kernel(
    field_ref, zt_hbm, send_ref, rows_hbm, rows_ref, zt_ref, coeff, stage, sems, zt_sems, out_sems,
):
    made = copies(field_ref, rows_ref, sems)
    step = 4
    zt_made = []
    for first in range(0, TILES, step):
        part = pl.ds(128 * first, 128 * step)
        zt_made += start_all((zt_hbm.at[part], zt_ref.at[part], zt_sems.at[first // step]))
        for copy in made[first * GROUPS : (first + step) * GROUPS]:
            copy.start()
    rows = rows_ref.reshape(TILES, ROWS, 128)
    kept = []
    for first in range(0, TILES, step):
        zt_made[first // step].wait()
        for copy in made[first * GROUPS : (first + step) * GROUPS]:
            copy.wait()
        some = pl.ds(first, step)
        kept += start_all((rows_ref.at[some], rows_hbm.at[some], out_sems.at[first // step]))
        part = jnp.concatenate([rows[t] for t in range(first, first + step)], axis=1)
        term = dot(part, zt_ref[pl.ds(128 * first, 128 * step), :])
        if first:
            coeff[...] += term
        else:
            coeff[...] = term
    pack_chunks(coeff, stage, jnp.zeros((DEV, 128), F32), send_ref)
    for copy in kept:
        copy.wait()


def weights_kernel(weight_ref, out_ref):
    gap = jnp.zeros((8, KY), F32)

    def one(o, carry):
        parts = []
        for s in range(Q3):
            for j in range(GROUPS):
                pieces = []
                for c in range(4):
                    pieces += [weight_ref[4 * j + c, o, s].astype(F32), gap]
                parts.append(jnp.concatenate(pieces, axis=0).T)
        out_ref[o] = jnp.concatenate(parts, axis=0).astype(BF16)
        return carry

    lax.fori_loop(0, C, one, 0)


def to_modes(recv_ref, x_ref, y_ref):
    pieces = recv_ref[...].reshape(PX, PY * CHUNK, 128)
    wide = jnp.concatenate([pieces[g] for g in range(PX)], axis=1)
    along = dot(wide, x_ref[...]).astype(BF16)
    tall = jnp.concatenate([along[:, :128], along[:, 128:]], axis=0)
    return dot(y_ref[...], tall).astype(BF16)


def from_modes(modes, y_ref, x_ref):
    tall = dot(y_ref[...], modes.astype(BF16), ((0,), (0,))).astype(BF16)
    half = PY * CHUNK
    wide = jnp.concatenate([tall[:half], tall[half:]], axis=1)
    return dot(wide, x_ref[...], ((1,), (1,)))


def pack_modes(spec):
    full = jnp.concatenate([spec, jnp.zeros((KY, 128), F32)], axis=0)
    last = full[3 * PACK :]
    inside = lax.broadcasted_iota(jnp.int32, (PACK, 128), 1) % 32 < KX
    parts = []
    for i in range(3):
        moved = pltpu.roll(last, KX - 8 * i, 1)
        parts.append(jnp.where(inside, full[PACK * i : PACK * (i + 1)], moved))
    return jnp.concatenate(parts, axis=0).astype(BF16)


def unpack_modes(packed):
    lane = lax.broadcasted_iota(jnp.int32, (PACK, 128), 1) % 32
    last = jnp.zeros((PACK, 128), F32)
    for i in range(3):
        part = packed[PACK * i : PACK * (i + 1)]
        moved = pltpu.roll(part, 128 - KX + 8 * i, 1)
        last = jnp.where((lane >= 8 * i) & (lane < 8 * (i + 1)), moved, last)
    return jnp.concatenate([packed, last], axis=0)


def write_chunks(values, send_ref):
    for g in range(PX):
        part = values[:, 128 * g : 128 * (g + 1)].astype(BF16)
        send_ref[pl.ds(g * PY, PY)] = part.reshape(PY, CHUNK, 128)


def mix_kernel(
    recv_ref, weight_ref, xa_ref, ya_ref, send_ref, spec_ref, modes,
):
    spec = to_modes(recv_ref, xa_ref, ya_ref).astype(F32)
    spec_ref[...] = pack_modes(spec)
    group = lax.broadcasted_iota(jnp.int32, (Q3 * KY, 128), 1) // 32
    for jo in range(GROUPS):
        total = jnp.zeros((Q3 * KY, 128), F32)
        for o4 in range(4):
            term = spec * weight_ref[4 * jo + o4].astype(F32)
            sums = []
            for s in range(Q3):
                at = s * GROUPS * KY
                acc = term[at : at + KY]
                for j in range(1, GROUPS):
                    acc = acc + term[at + j * KY : at + (j + 1) * KY]
                sums.append(acc)
            summed = jnp.concatenate(sums, axis=0)
            summed = summed + pltpu.roll(summed, 64, 1)
            summed = summed + pltpu.roll(summed, 32, 1)
            total = jnp.where(group == o4, summed, total)
        for s in range(Q3):
            modes[pl.ds((s * GROUPS + jo) * KY, KY), :] = total[s * KY : (s + 1) * KY]
    write_chunks(from_modes(modes[...], ya_ref, xa_ref), send_ref)


def mix_back_kernel(
    recv_ref, weight_ref, xa_ref, ya_ref, send_ref, spec_ref, stage,
):
    spec = to_modes(recv_ref, xa_ref, ya_ref)
    spec_ref[...] = pack_modes(spec.astype(F32))
    row = lax.broadcasted_iota(jnp.int32, (128, 512), 0)
    column = lax.broadcasted_iota(jnp.int32, (128, 512), 1)
    spread = (row // 32 == column // 128) & (row % 32 == column % 32)
    copied = dot(spec, spread.astype(F32).astype(BF16))
    modes = [jnp.zeros((KY, 128), F32) for _ in range(Q3 * GROUPS)]
    for o in range(C):
        weight = weight_ref[o].astype(F32)
        for s in range(Q3):
            at = (s * GROUPS + o // 4) * KY
            source = copied[at : at + KY, 128 * (o % 4) : 128 * (o % 4 + 1)]
            for j in range(GROUPS):
                k = s * GROUPS + j
                modes[k] = modes[k] + weight[k * KY : (k + 1) * KY] * source
    values = from_modes(jnp.concatenate(modes, axis=0), ya_ref, xa_ref)
    stage[...] = recv_ref[...].reshape(DEV * CHUNK, 128).astype(F32)
    extra = stage[pl.ds(CHUNK - 1, DEV, stride=CHUNK), :]
    extra = jnp.broadcast_to(jnp.sum(extra, axis=0, keepdims=True), (8, 128))
    extra = split_three(join_three(extra))[:1]
    row = lax.broadcasted_iota(jnp.int32, values.shape, 0) % CHUNK
    extra = jnp.concatenate([extra] * PX, axis=1)
    write_chunks(jnp.where(row == CHUNK - 1, extra, values), send_ref)


def block_of(ref, first, b):
    tiles = []
    for t in range(PER):
        rows = [ref[first + t, pl.ds(j * 128 + b * PART, PART), :] for j in range(GROUPS)]
        tiles.append(jnp.concatenate(rows, axis=0))
    return jnp.concatenate(tiles, axis=1)


def block_store(ref, first, b, value):
    for t in range(PER):
        for j in range(GROUPS):
            ref[first + t, pl.ds(j * 128 + b * PART, PART), :] = value[
                PART * j : PART * (j + 1), 128 * t : 128 * (t + 1)
            ]


def bypass_matrix(bypass_ref, channel_ref, same_ref, form, left_ref):
    half = dot(channel_ref[...], bypass_ref[...], form).astype(BF16)
    shifted = jnp.concatenate([jnp.zeros((64, C), F32), channel_ref[...].astype(F32)], axis=0)
    whole = dot(half, shifted.astype(BF16), ((1,), (1,)))
    whole = (whole * same_ref[...].astype(F32)).astype(BF16)
    for b in range(CX // XB):
        left_ref[b, :, pl.ds(128, BLOCK + 64)] = whole


K0 = math.sqrt(2.0 / math.pi)
K1 = 0.044715


def gelu_slope(x):
    square = x * x
    bend = jnp.tanh(x * (K0 + (K0 * K1) * square))
    inner = x * (K0 + (3.0 * K0 * K1) * square)
    return (0.5 + 0.5 * bend) * (1.0 + inner * (1.0 - bend))


def point_kernel(
    recv_ref, field_hbm, cot_hbm, bypass_ref, channel_ref, same_ref, back_ref, ahead_ref,
    send_ref, up_hbm, field_ref, cot_cells, up_ref, stage, left, coeff, cross, sems, cot_sems,
):
    field_hbm = field_hbm.reshape(TILES, ROWS, 128)
    cot_ref = cot_cells.reshape(TILES, ROWS, 128)
    cot_made = copies(cot_hbm, cot_cells, cot_sems)
    made = []
    for n in range(STEPS):
        some = pl.ds(PER * n, PER)
        made.append(start_all((field_hbm.at[some], field_ref.at[some], sems.at[1, n])))
        made[n] += cot_made[PER * n * GROUPS : PER * (n + 1) * GROUPS]
        for copy in made[n][1:]:
            copy.start()
    bypass_matrix(bypass_ref, channel_ref, same_ref, ((1,), (1,)), left)
    unpack_chunks(recv_ref, stage, left)
    coeff[...] = jnp.zeros_like(coeff)
    cross[...] = jnp.zeros_like(cross)
    kept = []
    for n in range(STEPS):
        for copy in made[n]:
            copy.wait()
        for b in range(CX // XB):
            cells = block_of(field_ref, PER * n, b)
            right = jnp.concatenate([back_ref[:, WIDE * n : WIDE * (n + 1)], cells], axis=0)
            pre = dot(left[b], right)
            slope = gelu_slope(pre) * block_of(cot_ref, PER * n, b).astype(F32)
            up = slope.astype(BF16)
            block_store(up_ref, PER * n, b, up)
            term = dot(up, ahead_ref[WIDE * n : WIDE * (n + 1), :])
            for j in range(GROUPS):
                coeff[pl.ds(j * 128 + b * PART, PART), :] += term[PART * j : PART * (j + 1)]
            cross[...] += dot(cells, up, ((1,), (1,)))
        some = pl.ds(PER * n, PER)
        kept += start_all((up_ref.at[some], up_hbm.at[some], sems.at[0, n]))
    kept_cross = cross[...] * same_ref[:, 64:].astype(F32)
    channel = channel_ref[...].astype(F32)
    high = lax.Precision.HIGHEST
    small = dot(dot(channel, kept_cross, ((0,), (0,)), high), channel, ((1,), (0,)), high)
    small = jnp.concatenate([small, jnp.zeros((C, 128 - C), F32)], axis=1)
    small = jnp.concatenate([small, jnp.zeros((DEV - C, 128), F32)], axis=0)
    pack_chunks(coeff, stage, split_three(small), send_ref)
    for copy in kept:
        copy.wait()


def final_kernel(
    recv_ref, up_hbm, bypass_ref, channel_ref, same_ref, back_hbm,
    out_ref, up_ref, back_ref, stage, left, rows_ref, table_sem, up_sems, sems,
):
    (table_made,) = start_all((back_hbm, back_ref, table_sem))
    up_made = []
    for n in range(STEPS):
        some = pl.ds(PER * n, PER)
        up_made += start_all((up_hbm.at[some], up_ref.at[some], up_sems.at[n]))
    bypass_matrix(bypass_ref, channel_ref, same_ref, ((1,), (0,)), left)
    unpack_chunks(recv_ref, stage, left)
    made = copies(out_ref, rows_ref, sems, back=True)
    rows = rows_ref.reshape(TILES, ROWS, 128)
    table_made.wait()
    for n in range(STEPS):
        up_made[n].wait()
        for b in range(CX // XB):
            cells = block_of(up_ref, PER * n, b)
            right = jnp.concatenate([back_ref[:, WIDE * n : WIDE * (n + 1)], cells], axis=0)
            block_store(rows, PER * n, b, dot(left[b], right).astype(BF16))
        for copy in made[PER * n * GROUPS : PER * (n + 1) * GROUPS]:
            copy.start()
    for copy in made:
        copy.wait()


def turn(value, b, tiles):
    for s in range(Q3):
        for j in range(GROUPS):
            at = (s * GROUPS + j) * KY
            turned = value[at : at + KY].T
            for c in range(4):
                tiles[4 * j + c, s, b] = turned[32 * c : 32 * c + KX]


PAIR = 4


def outer_kernel(*refs):
    out_ref, first, second = refs[8:]

    @pl.when(pl.program_id(0) == 0)
    def _():
        for b in range(4):
            turn(unpack_modes(refs[b][...].astype(F32)), b, first)
            turn(unpack_modes(refs[4 + b][...].astype(F32)), b, second)

    c = pl.program_id(0) * PAIR
    for s in range(Q3):
        own = [[first[c + i, s, b] for b in range(4)] for i in range(PAIR)]
        for o in range(C):
            other = [second[o, s, b] for b in range(4)]
            for i in range(PAIR):
                terms = [own[i][b] * other[b] for b in range(4)]
                out_ref[i, o, s] = (terms[0] + terms[2]) + (terms[1] + terms[3])


def small_kernel(recv_ref, small_ref, stage):
    stage[...] = recv_ref[pl.ds(0, 24)].astype(F32)
    small_ref[...] = join_three(stage[:, CHUNK - 1, :])


def call(kernel, out, in_specs, scratch, limit=12, **more):
    return pl.pallas_call(
        kernel,
        out_shape=out,
        in_specs=in_specs,
        scratch_shapes=scratch,
        compiler_params=pltpu.CompilerParams(vmem_limit_bytes=limit * MIB),
        **more,
    )


def around(value):
    return [value] + [
        lax.ppermute(value, "dp", [(i, (i + k) % 4) for i in range(4)]) for k in (1, 2, 3)
    ]


def body(field, cotangent, spectral_weight, bypass_weight):
    table = {name: jnp.asarray(value) for name, value in TABLES.items()}
    shape = jax.ShapeDtypeStruct
    chunks = shape((DEV, CHUNK, 128), BF16)
    cells = shape((TILES, GROUPS, CX, 4, CY, 128), BF16)
    rows = shape((TILES, ROWS, 128), BF16)
    stage = pltpu.VMEM((DEV * CHUNK, 128), F32)
    dma = lambda *count: pltpu.SemaphoreType.DMA(count)
    sems = dma(TILES, GROUPS)
    field_t = jnp.transpose(field[0], (0, 2, 1, 3))
    cot_t = jnp.transpose(cotangent[0], (0, 2, 1, 3))
    weight_t = jnp.transpose(spectral_weight, (2, 3, 4, 0, 1))

    def exchange(value):
        return lax.all_to_all(value, ("gx", "gy"), 0, 0, tiled=True)

    send, field_rows = call(
        analyze_kernel, (chunks, cells), [HBM, HBM],
        [pltpu.VMEM(cells.shape, BF16), pltpu.VMEM((NP, 256), BF16),
         pltpu.VMEM((ROWS, 256), F32), stage, sems, dma(4), dma(4)],
        out_specs=(VMEM, HBM), limit=62,
    )(field_t, table["zt_ahead"])
    recv = exchange(send)
    weight = call(
        weights_kernel, shape((C, SPEC, 128), BF16), [VMEM], [], out_specs=VMEM,
    )(weight_t)
    send, own = call(
        mix_kernel, (chunks, shape((3 * PACK, 128), BF16)), [VMEM] * 4,
        [pltpu.VMEM((SPEC, 128), F32)], out_specs=(VMEM,) * 2, limit=12,
    )(recv, weight, table["x_ahead"], table["y_ahead"])
    recv = exchange(send)
    left = pltpu.VMEM((CX // XB, BLOCK, NQ + BLOCK), BF16)
    held = pltpu.VMEM(rows.shape, BF16)
    back = pltpu.VMEM((NQ, NP), BF16)
    send, up = call(
        point_kernel, (chunks, rows), [VMEM, HBM, HBM] + [VMEM] * 5,
        [held, pltpu.VMEM(cells.shape, BF16), held, stage, left, pltpu.VMEM((ROWS, 256), F32),
         pltpu.VMEM((BLOCK, BLOCK), F32), dma(2, STEPS), sems],
        out_specs=(VMEM, HBM), limit=51,
    )(recv, field_rows, cot_t, bypass_weight, table["channel"], table["same"],
      table["zt_back"], table["zt_ahead"])
    recv = exchange(send)
    specs = around(own)
    recv, *specs = lax.optimization_barrier((recv, *specs))
    send, spec_up = call(
        mix_back_kernel, (chunks, shape((3 * PACK, 128), BF16)), [VMEM] * 4, [stage],
        out_specs=(VMEM,) * 2,
    )(recv, weight, table["x_ahead"], table["y_ahead"])
    recv = exchange(send)
    specs += around(spec_up)
    grad_spectral = pl.pallas_call(
        outer_kernel,
        grid=(C // PAIR,),
        out_shape=shape((C, C, Q3, KX, KY), F32),
        in_specs=[VMEM] * 8,
        out_specs=pl.BlockSpec((PAIR, C, Q3, KX, KY), lambda c: (c, 0, 0, 0, 0)),
        scratch_shapes=[pltpu.VMEM((C, Q3, 4, KX, KY), F32)] * 2,
        compiler_params=pltpu.CompilerParams(vmem_limit_bytes=24 * MIB),
        cost_estimate=pl.CostEstimate(
            flops=10**9, bytes_accessed=10**8, transcendentals=0
        ),
    )(*specs)
    recv, grad_spectral = lax.optimization_barrier((recv, grad_spectral))
    small = call(
        small_kernel, shape((24, 128), F32), [VMEM], [pltpu.VMEM((24, CHUNK, 128), F32)],
        out_specs=VMEM,
    )(recv)
    smalls = around(small)
    grad_field = call(
        final_kernel, shape((CX, C, CY, NP), BF16), [VMEM, HBM, VMEM, VMEM, VMEM, HBM],
        [held, back, stage, left, pltpu.VMEM(cells.shape, BF16), pltpu.SemaphoreType.DMA,
         dma(STEPS), sems],
        out_specs=HBM, limit=60,
    )(recv, up, bypass_weight, table["channel"], table["same"], table["zt_back"])
    grad_bypass = ((smalls[0] + smalls[2]) + (smalls[1] + smalls[3]))[:C, :C]
    return (
        jnp.transpose(grad_field, (0, 2, 1, 3))[None],
        jnp.transpose(grad_spectral, (3, 4, 0, 1, 2)),
        grad_bypass,
    )


def solution(mesh):
    in_specs = (
        P("dp", "gx", "gy", None, None),
        P("dp", "gx", "gy", None, None),
        P(None, None, None, None, ("gx", "gy")),
        P(),
    )
    out_specs = (P("dp", "gx", "gy", None, None), P(None, None, None, None, ("gx", "gy")), P())
    return jax.shard_map(body, mesh=mesh, in_specs=in_specs, out_specs=out_specs, check_vma=False)
```

```python
import math

import jax
import jax.numpy as jnp
import ml_dtypes
import numpy as np
from jax import lax
from jax.experimental import pallas as pl
from jax.experimental.pallas import tpu as pltpu
from jax.sharding import PartitionSpec as P

MX = 12
MY = 12
MZ = 12
MT = 4
NZ = 128
NT = 16
NX = 64
NY = 32
C = 20
KX = 2 * MX
KY = 2 * MY
PX = 4
PY = 16
DEV = PX * PY
CX = NX // PX
CY = NY // PY
NP = NZ * NT
TILES = NP // 128
GROUPS = C // 4
ROWS = C * CX * CY
Q3 = 3
CHUNK = 16
SPEC = Q3 * GROUPS * KY
PACK = (SPEC + KY) // 4
XB = 8
PART = 4 * XB * CY
WIDE = 512
STEPS = NP // WIDE
PER = WIDE // 128
NQ = Q3 * DEV
BLOCK = C * XB * CY
F32 = jnp.float32
BF16 = jnp.bfloat16
MIB = 2**20
VMEM = pl.BlockSpec(memory_space=pltpu.VMEM)
HBM = pl.BlockSpec(memory_space=pl.ANY)


def basis(length, kept):
    places = np.arange(length)[:, None]
    orders = np.arange(kept)[None, :]
    cos_part = np.cos(2 * np.pi * ((places * orders) % length) / length)
    sin_part = np.sin(2 * np.pi * ((places * (orders + 1)) % length) / length)
    return np.concatenate([cos_part, sin_part], axis=1) * math.sqrt(2.0 / length)


def tables():
    fx, fy = basis(NX, MX), basis(NY, MY)
    fzt = (basis(NZ, MZ)[:, None, :, None] * basis(NT, MT)[None, :, None, :]).reshape(NP, -1)
    by_slot = fzt.reshape(NP, DEV, Q3).transpose(0, 2, 1).reshape(NP, Q3 * DEV)
    ahead = np.zeros((NP, 256))
    ahead[:, : Q3 * DEV] = by_slot
    eye4, eye2 = np.eye(4), np.eye(CY)
    slots = np.eye(CHUNK)[:, : Q3 * GROUPS]
    fx32 = np.zeros((NX, 32))
    fx32[:, :KX] = fx
    x_ahead = np.einsum(
        "gxk,cd,yz->gxcyzdk", fx32.reshape(PX, CX, 32), eye4, eye2
    ).reshape(PX * 128, CY * 128)
    y_ahead = np.einsum("gyl,rs->slygr", fy.reshape(PY, CY, KY), slots).reshape(
        SPEC, CY * PY * CHUNK
    )
    channel = np.einsum("jk,x,cd,y->jxcykd", np.eye(GROUPS), np.ones(XB), eye4, np.ones(CY))
    channel = channel.reshape(BLOCK, C)
    cell = np.einsum("j,xw,c,yz->jxcywz", np.ones(GROUPS), np.eye(XB), np.ones(4), eye2)
    cell = cell.reshape(BLOCK, XB * CY)
    return {
        "zt_ahead": ahead,
        "zt_back": by_slot.T,
        "x_ahead": x_ahead,
        "y_ahead": y_ahead,
        "channel": channel,
        "same": np.concatenate([np.zeros((BLOCK, 64)), cell @ cell.T], axis=1),
    }


TABLES = {name: value.astype(ml_dtypes.bfloat16) for name, value in tables().items()}


def dot(a, b, form=((1,), (0,)), precision=None):
    return lax.dot_general(
        a, b, (form, ((), ())), preferred_element_type=F32, precision=precision
    )


def copies(field_ref, rows_ref, sems, back=False, tiles=range(TILES)):
    made = []
    for tile in tiles:
        for j in range(GROUPS):
            outer = field_ref.at[:, pl.ds(4 * j, 4), :, pl.ds(128 * tile, 128)]
            inner = rows_ref.at[tile, j]
            pair = (inner, outer) if back else (outer, inner)
            made.append(pltpu.make_async_copy(*pair, sems.at[tile, j]))
    return made


def pack_chunks(coeff_ref, stage, extra, send_ref):
    for j in range(GROUPS):
        turned = coeff_ref[pl.ds(128 * j, 128), :].T
        for s in range(Q3):
            stage[pl.ds(s * GROUPS + j, DEV, stride=CHUNK), :] = turned[s * DEV : (s + 1) * DEV]
    stage[pl.ds(CHUNK - 1, DEV, stride=CHUNK), :] = extra
    send_ref[...] = stage[...].astype(BF16).reshape(DEV, CHUNK, 128)


def unpack_chunks(recv_ref, stage, left_ref):
    stage[...] = recv_ref[...].reshape(DEV * CHUNK, 128).astype(F32)
    for j in range(GROUPS):
        parts = [stage[pl.ds(s * GROUPS + j, DEV, stride=CHUNK), :] for s in range(Q3)]
        turned = jnp.concatenate(parts, axis=0).T.astype(BF16)
        for b in range(CX // XB):
            left_ref[b, pl.ds(PART * j, PART), pl.ds(0, NQ)] = turned[PART * b : PART * (b + 1)]


def split_three(value):
    high = value.astype(BF16).astype(F32)
    rest = value - high
    middle = rest.astype(BF16).astype(F32)
    low = (rest - middle).astype(BF16).astype(F32)
    return high + pltpu.roll(middle, 32, 1) + pltpu.roll(low, 64, 1)


def join_three(value):
    lanes = lax.broadcasted_iota(jnp.int32, value.shape, 1)
    whole = value + (pltpu.roll(value, 96, 1) + pltpu.roll(value, 64, 1))
    return jnp.where(lanes < 32, whole, 0.0)


def start_all(*pairs):
    made = [pltpu.make_async_copy(*pair) for pair in pairs]
    for copy in made:
        copy.start()
    return made


def analyze_kernel(
    field_ref, zt_hbm, send_ref, rows_hbm, rows_ref, zt_ref, coeff, stage, sems, zt_sems, out_sems,
):
    made = copies(field_ref, rows_ref, sems)
    step = 4
    zt_made = []
    for first in range(0, TILES, step):
        part = pl.ds(128 * first, 128 * step)
        zt_made += start_all((zt_hbm.at[part], zt_ref.at[part], zt_sems.at[first // step]))
        for copy in made[first * GROUPS : (first + step) * GROUPS]:
            copy.start()
    rows = rows_ref.reshape(TILES, ROWS, 128)
    kept = []
    for first in range(0, TILES, step):
        zt_made[first // step].wait()
        for copy in made[first * GROUPS : (first + step) * GROUPS]:
            copy.wait()
        some = pl.ds(first, step)
        kept += start_all((rows_ref.at[some], rows_hbm.at[some], out_sems.at[first // step]))
        part = jnp.concatenate([rows[t] for t in range(first, first + step)], axis=1)
        term = dot(part, zt_ref[pl.ds(128 * first, 128 * step), :])
        if first:
            coeff[...] += term
        else:
            coeff[...] = term
    pack_chunks(coeff, stage, jnp.zeros((DEV, 128), F32), send_ref)
    for copy in kept:
        copy.wait()


def weights_kernel(weight_ref, out_ref):
    gap = jnp.zeros((8, KY), F32)

    def one(o, carry):
        parts = []
        for s in range(Q3):
            for j in range(GROUPS):
                pieces = []
                for c in range(4):
                    pieces += [weight_ref[4 * j + c, o, s].astype(F32), gap]
                parts.append(jnp.concatenate(pieces, axis=0).T)
        out_ref[o] = jnp.concatenate(parts, axis=0).astype(BF16)
        return carry

    lax.fori_loop(0, C, one, 0)


HALF = TILES // 2


def half_kernel(cot_ref, half_hbm, half_ref, sems, out_sem):
    made = copies(cot_ref, half_ref, sems, tiles=range(HALF))
    for copy in made:
        copy.start()
    for copy in made:
        copy.wait()
    for copy in start_all((half_ref, half_hbm, out_sem)):
        copy.wait()


def to_modes(recv_ref, x_ref, y_ref):
    pieces = recv_ref[...].reshape(PX, PY * CHUNK, 128)
    wide = jnp.concatenate([pieces[g] for g in range(PX)], axis=1)
    along = dot(wide, x_ref[...]).astype(BF16)
    tall = jnp.concatenate([along[:, :128], along[:, 128:]], axis=0)
    return dot(y_ref[...], tall).astype(BF16)


def from_modes(modes, y_ref, x_ref):
    tall = dot(y_ref[...], modes.astype(BF16), ((0,), (0,))).astype(BF16)
    half = PY * CHUNK
    wide = jnp.concatenate([tall[:half], tall[half:]], axis=1)
    return dot(wide, x_ref[...], ((1,), (1,)))


def pack_modes(spec):
    full = jnp.concatenate([spec, jnp.zeros((KY, 128), F32)], axis=0)
    last = full[3 * PACK :]
    inside = lax.broadcasted_iota(jnp.int32, (PACK, 128), 1) % 32 < KX
    parts = []
    for i in range(3):
        moved = pltpu.roll(last, KX - 8 * i, 1)
        parts.append(jnp.where(inside, full[PACK * i : PACK * (i + 1)], moved))
    return jnp.concatenate(parts, axis=0).astype(BF16)


def unpack_modes(packed):
    lane = lax.broadcasted_iota(jnp.int32, (PACK, 128), 1) % 32
    last = jnp.zeros((PACK, 128), F32)
    for i in range(3):
        part = packed[PACK * i : PACK * (i + 1)]
        moved = pltpu.roll(part, 128 - KX + 8 * i, 1)
        last = jnp.where((lane >= 8 * i) & (lane < 8 * (i + 1)), moved, last)
    return jnp.concatenate([packed, last], axis=0)


def write_chunks(values, send_ref):
    for g in range(PX):
        part = values[:, 128 * g : 128 * (g + 1)].astype(BF16)
        send_ref[pl.ds(g * PY, PY)] = part.reshape(PY, CHUNK, 128)


def mix_kernel(
    recv_ref, weight_ref, xa_ref, ya_ref, send_ref, spec_ref, modes,
):
    spec = to_modes(recv_ref, xa_ref, ya_ref).astype(F32)
    spec_ref[...] = pack_modes(spec)
    group = lax.broadcasted_iota(jnp.int32, (Q3 * KY, 128), 1) // 32
    for jo in range(GROUPS):
        total = jnp.zeros((Q3 * KY, 128), F32)
        for o4 in range(4):
            term = spec * weight_ref[4 * jo + o4].astype(F32)
            sums = []
            for s in range(Q3):
                at = s * GROUPS * KY
                acc = term[at : at + KY]
                for j in range(1, GROUPS):
                    acc = acc + term[at + j * KY : at + (j + 1) * KY]
                sums.append(acc)
            summed = jnp.concatenate(sums, axis=0)
            summed = summed + pltpu.roll(summed, 64, 1)
            summed = summed + pltpu.roll(summed, 32, 1)
            total = jnp.where(group == o4, summed, total)
        for s in range(Q3):
            modes[pl.ds((s * GROUPS + jo) * KY, KY), :] = total[s * KY : (s + 1) * KY]
    write_chunks(from_modes(modes[...], ya_ref, xa_ref), send_ref)


def mix_back_kernel(
    recv_ref, weight_ref, xa_ref, ya_ref, send_ref, spec_ref, stage,
):
    spec = to_modes(recv_ref, xa_ref, ya_ref)
    spec_ref[...] = pack_modes(spec.astype(F32))
    row = lax.broadcasted_iota(jnp.int32, (128, 512), 0)
    column = lax.broadcasted_iota(jnp.int32, (128, 512), 1)
    spread = (row // 32 == column // 128) & (row % 32 == column % 32)
    copied = dot(spec, spread.astype(F32).astype(BF16))
    modes = [jnp.zeros((KY, 128), F32) for _ in range(Q3 * GROUPS)]
    for o in range(C):
        weight = weight_ref[o].astype(F32)
        for s in range(Q3):
            at = (s * GROUPS + o // 4) * KY
            source = copied[at : at + KY, 128 * (o % 4) : 128 * (o % 4 + 1)]
            for j in range(GROUPS):
                k = s * GROUPS + j
                modes[k] = modes[k] + weight[k * KY : (k + 1) * KY] * source
    values = from_modes(jnp.concatenate(modes, axis=0), ya_ref, xa_ref)
    stage[...] = recv_ref[...].reshape(DEV * CHUNK, 128).astype(F32)
    extra = stage[pl.ds(CHUNK - 1, DEV, stride=CHUNK), :]
    extra = jnp.broadcast_to(jnp.sum(extra, axis=0, keepdims=True), (8, 128))
    extra = split_three(join_three(extra))[:1]
    row = lax.broadcasted_iota(jnp.int32, values.shape, 0) % CHUNK
    extra = jnp.concatenate([extra] * PX, axis=1)
    write_chunks(jnp.where(row == CHUNK - 1, extra, values), send_ref)


def block_of(ref, first, b):
    tiles = []
    for t in range(PER):
        rows = [ref[first + t, pl.ds(j * 128 + b * PART, PART), :] for j in range(GROUPS)]
        tiles.append(jnp.concatenate(rows, axis=0))
    return jnp.concatenate(tiles, axis=1)


def block_store(ref, first, b, value):
    for t in range(PER):
        for j in range(GROUPS):
            ref[first + t, pl.ds(j * 128 + b * PART, PART), :] = value[
                PART * j : PART * (j + 1), 128 * t : 128 * (t + 1)
            ]


def bypass_matrix(bypass_ref, channel_ref, same_ref, form, left_ref):
    half = dot(channel_ref[...], bypass_ref[...], form).astype(BF16)
    shifted = jnp.concatenate([jnp.zeros((64, C), F32), channel_ref[...].astype(F32)], axis=0)
    whole = dot(half, shifted.astype(BF16), ((1,), (1,)))
    whole = (whole * same_ref[...].astype(F32)).astype(BF16)
    for b in range(CX // XB):
        left_ref[b, :, pl.ds(128, BLOCK + 64)] = whole


K0 = math.sqrt(2.0 / math.pi)
K1 = 0.044715


def gelu_slope(x):
    square = x * x
    bend = jnp.tanh(x * (K0 + (K0 * K1) * square))
    inner = x * (K0 + (3.0 * K0 * K1) * square)
    return (0.5 + 0.5 * bend) * (1.0 + inner * (1.0 - bend))


def point_kernel(
    recv_ref, field_hbm, half_hbm, cot_hbm, bypass_ref, channel_ref, same_ref, back_ref, ahead_ref,
    send_ref, up_hbm, field_ref, cot_cells, up_ref, stage, left, coeff, cross, sems, cot_sems,
):
    field_hbm = field_hbm.reshape(TILES, ROWS, 128)
    cot_ref = cot_cells.reshape(TILES, ROWS, 128)
    half_hbm = half_hbm.reshape(HALF, ROWS, 128)
    cot_made = copies(cot_hbm, cot_cells, cot_sems, tiles=range(HALF, TILES))
    made = []
    for n in range(STEPS):
        some = pl.ds(PER * n, PER)
        made.append(start_all((field_hbm.at[some], field_ref.at[some], sems.at[1, n])))
        if PER * n < HALF:
            made[n] += start_all((half_hbm.at[some], cot_ref.at[some], cot_sems.at[PER * n, 0]))
        else:
            at = (PER * n - HALF) * GROUPS
            made[n] += cot_made[at : at + PER * GROUPS]
            for copy in made[n][1:]:
                copy.start()
    bypass_matrix(bypass_ref, channel_ref, same_ref, ((1,), (1,)), left)
    unpack_chunks(recv_ref, stage, left)
    coeff[...] = jnp.zeros_like(coeff)
    cross[...] = jnp.zeros_like(cross)
    kept = []
    for n in range(STEPS):
        for copy in made[n]:
            copy.wait()
        for b in range(CX // XB):
            cells = block_of(field_ref, PER * n, b)
            right = jnp.concatenate([back_ref[:, WIDE * n : WIDE * (n + 1)], cells], axis=0)
            pre = dot(left[b], right)
            slope = gelu_slope(pre) * block_of(cot_ref, PER * n, b).astype(F32)
            up = slope.astype(BF16)
            block_store(up_ref, PER * n, b, up)
            term = dot(up, ahead_ref[WIDE * n : WIDE * (n + 1), :])
            for j in range(GROUPS):
                coeff[pl.ds(j * 128 + b * PART, PART), :] += term[PART * j : PART * (j + 1)]
            cross[...] += dot(cells, up, ((1,), (1,)))
        some = pl.ds(PER * n, PER)
        kept += start_all((up_ref.at[some], up_hbm.at[some], sems.at[0, n]))
    kept_cross = cross[...] * same_ref[:, 64:].astype(F32)
    channel = channel_ref[...].astype(F32)
    high = lax.Precision.HIGHEST
    small = dot(dot(channel, kept_cross, ((0,), (0,)), high), channel, ((1,), (0,)), high)
    small = jnp.concatenate([small, jnp.zeros((C, 128 - C), F32)], axis=1)
    small = jnp.concatenate([small, jnp.zeros((DEV - C, 128), F32)], axis=0)
    pack_chunks(coeff, stage, split_three(small), send_ref)
    for copy in kept:
        copy.wait()


def final_kernel(
    recv_ref, up_hbm, bypass_ref, channel_ref, same_ref, back_hbm,
    out_ref, up_ref, back_ref, stage, left, rows_ref, table_sem, up_sems, sems,
):
    (table_made,) = start_all((back_hbm, back_ref, table_sem))
    up_made = []
    for n in range(STEPS):
        some = pl.ds(PER * n, PER)
        up_made += start_all((up_hbm.at[some], up_ref.at[some], up_sems.at[n]))
    bypass_matrix(bypass_ref, channel_ref, same_ref, ((1,), (0,)), left)
    unpack_chunks(recv_ref, stage, left)
    made = copies(out_ref, rows_ref, sems, back=True)
    rows = rows_ref.reshape(TILES, ROWS, 128)
    table_made.wait()
    for n in range(STEPS):
        up_made[n].wait()
        for b in range(CX // XB):
            cells = block_of(up_ref, PER * n, b)
            right = jnp.concatenate([back_ref[:, WIDE * n : WIDE * (n + 1)], cells], axis=0)
            block_store(rows, PER * n, b, dot(left[b], right).astype(BF16))
        for copy in made[PER * n * GROUPS : PER * (n + 1) * GROUPS]:
            copy.start()
    for copy in made:
        copy.wait()


def turn(value, b, tiles):
    for s in range(Q3):
        for j in range(GROUPS):
            at = (s * GROUPS + j) * KY
            turned = value[at : at + KY].T
            for c in range(4):
                tiles[4 * j + c, s, b] = turned[32 * c : 32 * c + KX]


PAIR = 4


def outer_kernel(*refs):
    out_ref, first, second = refs[8:]

    @pl.when(pl.program_id(0) == 0)
    def _():
        for b in range(4):
            turn(unpack_modes(refs[b][...].astype(F32)), b, first)
            turn(unpack_modes(refs[4 + b][...].astype(F32)), b, second)

    c = pl.program_id(0) * PAIR
    for s in range(Q3):
        own = [[first[c + i, s, b] for b in range(4)] for i in range(PAIR)]
        for o in range(C):
            other = [second[o, s, b] for b in range(4)]
            for i in range(PAIR):
                terms = [own[i][b] * other[b] for b in range(4)]
                out_ref[i, o, s] = (terms[0] + terms[2]) + (terms[1] + terms[3])


def small_kernel(recv_ref, small_ref, stage):
    stage[...] = recv_ref[pl.ds(0, 24)].astype(F32)
    small_ref[...] = join_three(stage[:, CHUNK - 1, :])


def call(kernel, out, in_specs, scratch, limit=12, **more):
    return pl.pallas_call(
        kernel,
        out_shape=out,
        in_specs=in_specs,
        scratch_shapes=scratch,
        compiler_params=pltpu.CompilerParams(vmem_limit_bytes=limit * MIB),
        **more,
    )


def around(value):
    return [value] + [
        lax.ppermute(value, "dp", [(i, (i + k) % 4) for i in range(4)]) for k in (1, 2, 3)
    ]


def body(field, cotangent, spectral_weight, bypass_weight):
    table = {name: jnp.asarray(value) for name, value in TABLES.items()}
    shape = jax.ShapeDtypeStruct
    chunks = shape((DEV, CHUNK, 128), BF16)
    cells = shape((TILES, GROUPS, CX, 4, CY, 128), BF16)
    rows = shape((TILES, ROWS, 128), BF16)
    stage = pltpu.VMEM((DEV * CHUNK, 128), F32)
    dma = lambda *count: pltpu.SemaphoreType.DMA(count)
    sems = dma(TILES, GROUPS)
    field_t = jnp.transpose(field[0], (0, 2, 1, 3))
    cot_t = jnp.transpose(cotangent[0], (0, 2, 1, 3))
    weight_t = jnp.transpose(spectral_weight, (2, 3, 4, 0, 1))

    def exchange(value):
        return lax.all_to_all(value, ("gx", "gy"), 0, 0, tiled=True)

    send, field_rows = call(
        analyze_kernel, (chunks, cells), [HBM, HBM],
        [pltpu.VMEM(cells.shape, BF16), pltpu.VMEM((NP, 256), BF16),
         pltpu.VMEM((ROWS, 256), F32), stage, sems, dma(4), dma(4)],
        out_specs=(VMEM, HBM), limit=62,
    )(field_t, table["zt_ahead"])
    recv = exchange(send)
    weight = call(
        weights_kernel, shape((C, SPEC, 128), BF16), [VMEM], [], out_specs=VMEM,
    )(weight_t)
    some = shape((HALF, GROUPS, CX, 4, CY, 128), BF16)
    half = call(
        half_kernel, some, [HBM],
        [pltpu.VMEM(some.shape, BF16), sems, pltpu.SemaphoreType.DMA], out_specs=HBM, limit=60,
    )(cot_t)
    weight, half = lax.optimization_barrier((weight, half))
    send, own = call(
        mix_kernel, (chunks, shape((3 * PACK, 128), BF16)), [VMEM] * 4,
        [pltpu.VMEM((SPEC, 128), F32)], out_specs=(VMEM,) * 2, limit=12,
    )(recv, weight, table["x_ahead"], table["y_ahead"])
    recv = exchange(send)
    left = pltpu.VMEM((CX // XB, BLOCK, NQ + BLOCK), BF16)
    held = pltpu.VMEM(rows.shape, BF16)
    back = pltpu.VMEM((NQ, NP), BF16)
    send, up = call(
        point_kernel, (chunks, rows), [VMEM] + [HBM] * 3 + [VMEM] * 5,
        [held, pltpu.VMEM(cells.shape, BF16), held, stage, left, pltpu.VMEM((ROWS, 256), F32),
         pltpu.VMEM((BLOCK, BLOCK), F32), dma(2, STEPS), sems],
        out_specs=(VMEM, HBM), limit=51,
    )(recv, field_rows, half, cot_t, bypass_weight, table["channel"], table["same"],
      table["zt_back"], table["zt_ahead"])
    recv = exchange(send)
    specs = around(own)
    recv, *specs = lax.optimization_barrier((recv, *specs))
    send, spec_up = call(
        mix_back_kernel, (chunks, shape((3 * PACK, 128), BF16)), [VMEM] * 4, [stage],
        out_specs=(VMEM,) * 2,
    )(recv, weight, table["x_ahead"], table["y_ahead"])
    recv = exchange(send)
    specs += around(spec_up)
    grad_spectral = pl.pallas_call(
        outer_kernel,
        grid=(C // PAIR,),
        out_shape=shape((C, C, Q3, KX, KY), F32),
        in_specs=[VMEM] * 8,
        out_specs=pl.BlockSpec((PAIR, C, Q3, KX, KY), lambda c: (c, 0, 0, 0, 0)),
        scratch_shapes=[pltpu.VMEM((C, Q3, 4, KX, KY), F32)] * 2,
        compiler_params=pltpu.CompilerParams(vmem_limit_bytes=24 * MIB),
        cost_estimate=pl.CostEstimate(
            flops=10**9, bytes_accessed=10**8, transcendentals=0
        ),
    )(*specs)
    recv, grad_spectral = lax.optimization_barrier((recv, grad_spectral))
    small = call(
        small_kernel, shape((24, 128), F32), [VMEM], [pltpu.VMEM((24, CHUNK, 128), F32)],
        out_specs=VMEM,
    )(recv)
    smalls = around(small)
    grad_field = call(
        final_kernel, shape((CX, C, CY, NP), BF16), [VMEM, HBM, VMEM, VMEM, VMEM, HBM],
        [held, back, stage, left, pltpu.VMEM(cells.shape, BF16), pltpu.SemaphoreType.DMA,
         dma(STEPS), sems],
        out_specs=HBM, limit=60,
    )(recv, up, bypass_weight, table["channel"], table["same"], table["zt_back"])
    grad_bypass = ((smalls[0] + smalls[2]) + (smalls[1] + smalls[3]))[:C, :C]
    return (
        jnp.transpose(grad_field, (0, 2, 1, 3))[None],
        jnp.transpose(grad_spectral, (3, 4, 0, 1, 2)),
        grad_bypass,
    )


def solution(mesh):
    in_specs = (
        P("dp", "gx", "gy", None, None),
        P("dp", "gx", "gy", None, None),
        P(None, None, None, None, ("gx", "gy")),
        P(),
    )
    out_specs = (P("dp", "gx", "gy", None, None), P(None, None, None, None, ("gx", "gy")), P())
    return jax.shard_map(body, mesh=mesh, in_specs=in_specs, out_specs=out_specs, check_vma=False)
```

```python
import math

import jax
import jax.numpy as jnp
import ml_dtypes
import numpy as np
from jax import lax
from jax.experimental import pallas as pl
from jax.experimental.pallas import tpu as pltpu
from jax.sharding import PartitionSpec as P

MX = 12
MY = 12
MZ = 12
MT = 4
NZ = 128
NT = 16
NX = 64
NY = 32
C = 20
KX = 2 * MX
KY = 2 * MY
PX = 4
PY = 16
DEV = PX * PY
CX = NX // PX
CY = NY // PY
NP = NZ * NT
TILES = NP // 128
GROUPS = C // 4
ROWS = C * CX * CY
Q3 = 3
CHUNK = 16
SPEC = Q3 * GROUPS * KY
PACK = (SPEC + KY) // 4
XB = 8
PART = 4 * XB * CY
WIDE = 512
STEPS = NP // WIDE
PER = WIDE // 128
NQ = Q3 * DEV
BLOCK = C * XB * CY
F32 = jnp.float32
BF16 = jnp.bfloat16
MIB = 2**20
VMEM = pl.BlockSpec(memory_space=pltpu.VMEM)
HBM = pl.BlockSpec(memory_space=pl.ANY)


def basis(length, kept):
    places = np.arange(length)[:, None]
    orders = np.arange(kept)[None, :]
    cos_part = np.cos(2 * np.pi * ((places * orders) % length) / length)
    sin_part = np.sin(2 * np.pi * ((places * (orders + 1)) % length) / length)
    return np.concatenate([cos_part, sin_part], axis=1) * math.sqrt(2.0 / length)


def tables():
    fx, fy = basis(NX, MX), basis(NY, MY)
    fzt = (basis(NZ, MZ)[:, None, :, None] * basis(NT, MT)[None, :, None, :]).reshape(NP, -1)
    by_slot = fzt.reshape(NP, DEV, Q3).transpose(0, 2, 1).reshape(NP, Q3 * DEV)
    ahead = np.zeros((NP, 256))
    ahead[:, : Q3 * DEV] = by_slot
    eye4, eye2 = np.eye(4), np.eye(CY)
    slots = np.eye(CHUNK)[:, : Q3 * GROUPS]
    fx32 = np.zeros((NX, 32))
    fx32[:, :KX] = fx
    x_ahead = np.einsum(
        "gxk,cd,yz->gxcyzdk", fx32.reshape(PX, CX, 32), eye4, eye2
    ).reshape(PX * 128, CY * 128)
    y_ahead = np.einsum("gyl,rs->slygr", fy.reshape(PY, CY, KY), slots).reshape(
        SPEC, CY * PY * CHUNK
    )
    channel = np.einsum("jk,x,cd,y->jxcykd", np.eye(GROUPS), np.ones(XB), eye4, np.ones(CY))
    channel = channel.reshape(BLOCK, C)
    cell = np.einsum("j,xw,c,yz->jxcywz", np.ones(GROUPS), np.eye(XB), np.ones(4), eye2)
    cell = cell.reshape(BLOCK, XB * CY)
    return {
        "zt_ahead": ahead,
        "zt_back": by_slot.T,
        "x_ahead": x_ahead,
        "y_ahead": y_ahead,
        "channel": channel,
        "same": np.concatenate([np.zeros((BLOCK, 64)), cell @ cell.T], axis=1),
    }


TABLES = {name: value.astype(ml_dtypes.bfloat16) for name, value in tables().items()}


def dot(a, b, form=((1,), (0,)), precision=None):
    return lax.dot_general(
        a, b, (form, ((), ())), preferred_element_type=F32, precision=precision
    )


def copies(field_ref, rows_ref, sems, back=False):
    made = []
    for tile in range(TILES):
        for j in range(GROUPS):
            outer = field_ref.at[:, pl.ds(4 * j, 4), :, pl.ds(128 * tile, 128)]
            inner = rows_ref.at[tile, j]
            pair = (inner, outer) if back else (outer, inner)
            made.append(pltpu.make_async_copy(*pair, sems.at[tile, j]))
    return made


def pack_chunks(coeff_ref, stage, extra, send_ref):
    for j in range(GROUPS):
        turned = coeff_ref[pl.ds(128 * j, 128), :].T
        for s in range(Q3):
            stage[pl.ds(s * GROUPS + j, DEV, stride=CHUNK), :] = turned[s * DEV : (s + 1) * DEV]
    stage[pl.ds(CHUNK - 1, DEV, stride=CHUNK), :] = extra
    send_ref[...] = stage[...].astype(BF16).reshape(DEV, CHUNK, 128)


def unpack_chunks(recv_ref, stage, left_ref):
    stage[...] = recv_ref[...].reshape(DEV * CHUNK, 128).astype(F32)
    for j in range(GROUPS):
        parts = [stage[pl.ds(s * GROUPS + j, DEV, stride=CHUNK), :] for s in range(Q3)]
        turned = jnp.concatenate(parts, axis=0).T.astype(BF16)
        for b in range(CX // XB):
            left_ref[b, pl.ds(PART * j, PART), pl.ds(0, NQ)] = turned[PART * b : PART * (b + 1)]


def split_three(value):
    high = value.astype(BF16).astype(F32)
    rest = value - high
    middle = rest.astype(BF16).astype(F32)
    low = (rest - middle).astype(BF16).astype(F32)
    return high + pltpu.roll(middle, 32, 1) + pltpu.roll(low, 64, 1)


def join_three(value):
    lanes = lax.broadcasted_iota(jnp.int32, value.shape, 1)
    whole = value + (pltpu.roll(value, 96, 1) + pltpu.roll(value, 64, 1))
    return jnp.where(lanes < 32, whole, 0.0)


def start_all(*pairs):
    made = [pltpu.make_async_copy(*pair) for pair in pairs]
    for copy in made:
        copy.start()
    return made


def analyze_kernel(
    field_ref, zt_hbm, send_ref, rows_hbm, rows_ref, zt_ref, coeff, stage, sems, zt_sems, out_sems,
):
    made = copies(field_ref, rows_ref, sems)
    step = 4
    zt_made = []
    for first in range(0, TILES, step):
        part = pl.ds(128 * first, 128 * step)
        zt_made += start_all((zt_hbm.at[part], zt_ref.at[part], zt_sems.at[first // step]))
        for copy in made[first * GROUPS : (first + step) * GROUPS]:
            copy.start()
    rows = rows_ref.reshape(TILES, ROWS, 128)
    kept = []
    for first in range(0, TILES, step):
        zt_made[first // step].wait()
        for copy in made[first * GROUPS : (first + step) * GROUPS]:
            copy.wait()
        some = pl.ds(first, step)
        kept += start_all((rows_ref.at[some], rows_hbm.at[some], out_sems.at[first // step]))
        part = jnp.concatenate([rows[t] for t in range(first, first + step)], axis=1)
        term = dot(part, zt_ref[pl.ds(128 * first, 128 * step), :])
        if first:
            coeff[...] += term
        else:
            coeff[...] = term
    pack_chunks(coeff, stage, jnp.zeros((DEV, 128), F32), send_ref)
    for copy in kept:
        copy.wait()


def weights_kernel(weight_ref, out_ref):
    gap = jnp.zeros((8, KY), F32)

    def one(o, carry):
        parts = []
        for s in range(Q3):
            for j in range(GROUPS):
                pieces = []
                for c in range(4):
                    pieces += [weight_ref[4 * j + c, o, s].astype(F32), gap]
                parts.append(jnp.concatenate(pieces, axis=0).T)
        out_ref[o] = jnp.concatenate(parts, axis=0).astype(BF16)
        return carry

    lax.fori_loop(0, C, one, 0)


def to_modes(recv_ref, x_ref, y_ref):
    pieces = recv_ref[...].reshape(PX, PY * CHUNK, 128)
    wide = jnp.concatenate([pieces[g] for g in range(PX)], axis=1)
    along = dot(wide, x_ref[...]).astype(BF16)
    tall = jnp.concatenate([along[:, :128], along[:, 128:]], axis=0)
    return dot(y_ref[...], tall).astype(BF16)


def from_modes(modes, y_ref, x_ref):
    tall = dot(y_ref[...], modes.astype(BF16), ((0,), (0,))).astype(BF16)
    half = PY * CHUNK
    wide = jnp.concatenate([tall[:half], tall[half:]], axis=1)
    return dot(wide, x_ref[...], ((1,), (1,)))


def pack_modes(spec):
    full = jnp.concatenate([spec, jnp.zeros((KY, 128), F32)], axis=0)
    last = full[3 * PACK :]
    inside = lax.broadcasted_iota(jnp.int32, (PACK, 128), 1) % 32 < KX
    parts = []
    for i in range(3):
        moved = pltpu.roll(last, KX - 8 * i, 1)
        parts.append(jnp.where(inside, full[PACK * i : PACK * (i + 1)], moved))
    return jnp.concatenate(parts, axis=0).astype(BF16)


def unpack_modes(packed):
    lane = lax.broadcasted_iota(jnp.int32, (PACK, 128), 1) % 32
    last = jnp.zeros((PACK, 128), F32)
    for i in range(3):
        part = packed[PACK * i : PACK * (i + 1)]
        moved = pltpu.roll(part, 128 - KX + 8 * i, 1)
        last = jnp.where((lane >= 8 * i) & (lane < 8 * (i + 1)), moved, last)
    return jnp.concatenate([packed, last], axis=0)


def write_chunks(values, send_ref):
    for g in range(PX):
        part = values[:, 128 * g : 128 * (g + 1)].astype(BF16)
        send_ref[pl.ds(g * PY, PY)] = part.reshape(PY, CHUNK, 128)


def mix_kernel(
    recv_ref, weight_ref, xa_ref, ya_ref, send_ref, spec_ref, modes,
):
    spec = to_modes(recv_ref, xa_ref, ya_ref).astype(F32)
    spec_ref[...] = pack_modes(spec)
    group = lax.broadcasted_iota(jnp.int32, (Q3 * KY, 128), 1) // 32
    for jo in range(GROUPS):
        total = jnp.zeros((Q3 * KY, 128), F32)
        for o4 in range(4):
            term = spec * weight_ref[4 * jo + o4].astype(F32)
            sums = []
            for s in range(Q3):
                at = s * GROUPS * KY
                acc = term[at : at + KY]
                for j in range(1, GROUPS):
                    acc = acc + term[at + j * KY : at + (j + 1) * KY]
                sums.append(acc)
            summed = jnp.concatenate(sums, axis=0)
            summed = summed + pltpu.roll(summed, 64, 1)
            summed = summed + pltpu.roll(summed, 32, 1)
            total = jnp.where(group == o4, summed, total)
        for s in range(Q3):
            modes[pl.ds((s * GROUPS + jo) * KY, KY), :] = total[s * KY : (s + 1) * KY]
    write_chunks(from_modes(modes[...], ya_ref, xa_ref), send_ref)


def mix_back_kernel(
    recv_ref, weight_ref, xa_ref, ya_ref, send_ref, spec_ref, stage,
):
    spec = to_modes(recv_ref, xa_ref, ya_ref)
    spec_ref[...] = pack_modes(spec.astype(F32))
    row = lax.broadcasted_iota(jnp.int32, (128, 512), 0)
    column = lax.broadcasted_iota(jnp.int32, (128, 512), 1)
    spread = (row // 32 == column // 128) & (row % 32 == column % 32)
    copied = dot(spec, spread.astype(F32).astype(BF16))
    modes = [jnp.zeros((KY, 128), F32) for _ in range(Q3 * GROUPS)]
    for o in range(C):
        weight = weight_ref[o].astype(F32)
        for s in range(Q3):
            at = (s * GROUPS + o // 4) * KY
            source = copied[at : at + KY, 128 * (o % 4) : 128 * (o % 4 + 1)]
            for j in range(GROUPS):
                k = s * GROUPS + j
                modes[k] = modes[k] + weight[k * KY : (k + 1) * KY] * source
    values = from_modes(jnp.concatenate(modes, axis=0), ya_ref, xa_ref)
    stage[...] = recv_ref[...].reshape(DEV * CHUNK, 128).astype(F32)
    extra = stage[pl.ds(CHUNK - 1, DEV, stride=CHUNK), :]
    extra = jnp.broadcast_to(jnp.sum(extra, axis=0, keepdims=True), (8, 128))
    extra = split_three(join_three(extra))[:1]
    row = lax.broadcasted_iota(jnp.int32, values.shape, 0) % CHUNK
    extra = jnp.concatenate([extra] * PX, axis=1)
    write_chunks(jnp.where(row == CHUNK - 1, extra, values), send_ref)


def block_of(ref, first, b):
    tiles = []
    for t in range(PER):
        rows = [ref[first + t, pl.ds(j * 128 + b * PART, PART), :] for j in range(GROUPS)]
        tiles.append(jnp.concatenate(rows, axis=0))
    return jnp.concatenate(tiles, axis=1)


def block_store(ref, first, b, value):
    for t in range(PER):
        for j in range(GROUPS):
            ref[first + t, pl.ds(j * 128 + b * PART, PART), :] = value[
                PART * j : PART * (j + 1), 128 * t : 128 * (t + 1)
            ]


def bypass_matrix(bypass_ref, channel_ref, same_ref, form, left_ref):
    half = dot(channel_ref[...], bypass_ref[...], form).astype(BF16)
    shifted = jnp.concatenate([jnp.zeros((64, C), F32), channel_ref[...].astype(F32)], axis=0)
    whole = dot(half, shifted.astype(BF16), ((1,), (1,)))
    whole = (whole * same_ref[...].astype(F32)).astype(BF16)
    for b in range(CX // XB):
        left_ref[b, :, pl.ds(128, BLOCK + 64)] = whole


K0 = math.sqrt(2.0 / math.pi)
K1 = 0.044715


def gelu_slope(x):
    square = x * x
    bend = jnp.tanh(x * (K0 + (K0 * K1) * square))
    inner = x * (K0 + (3.0 * K0 * K1) * square)
    return (0.5 + 0.5 * bend) * (1.0 + inner * (1.0 - bend))


def point_kernel(
    recv_ref, field_hbm, cot_hbm, bypass_ref, channel_ref, same_ref, back_ref, ahead_ref,
    send_ref, up_hbm, field_ref, cot_cells, up_ref, stage, left, coeff, cross, sems, cot_sems,
):
    field_hbm = field_hbm.reshape(TILES, ROWS, 128)
    cot_ref = cot_cells.reshape(TILES, ROWS, 128)
    cot_made = copies(cot_hbm, cot_cells, cot_sems)
    made = []
    for n in range(STEPS):
        some = pl.ds(PER * n, PER)
        made.append(start_all((field_hbm.at[some], field_ref.at[some], sems.at[1, n])))
        made[n] += cot_made[PER * n * GROUPS : PER * (n + 1) * GROUPS]
        for copy in made[n][1:]:
            copy.start()
    bypass_matrix(bypass_ref, channel_ref, same_ref, ((1,), (1,)), left)
    unpack_chunks(recv_ref, stage, left)
    coeff[...] = jnp.zeros_like(coeff)
    cross[...] = jnp.zeros_like(cross)
    kept = []
    for n in range(STEPS):
        for copy in made[n]:
            copy.wait()
        for b in range(CX // XB):
            cells = block_of(field_ref, PER * n, b)
            right = jnp.concatenate([back_ref[:, WIDE * n : WIDE * (n + 1)], cells], axis=0)
            pre = dot(left[b], right)
            slope = gelu_slope(pre) * block_of(cot_ref, PER * n, b).astype(F32)
            up = slope.astype(BF16)
            block_store(up_ref, PER * n, b, up)
            term = dot(up, ahead_ref[WIDE * n : WIDE * (n + 1), :])
            for j in range(GROUPS):
                coeff[pl.ds(j * 128 + b * PART, PART), :] += term[PART * j : PART * (j + 1)]
            cross[...] += dot(cells, up, ((1,), (1,)))
        some = pl.ds(PER * n, PER)
        kept += start_all((up_ref.at[some], up_hbm.at[some], sems.at[0, n]))
    kept_cross = cross[...] * same_ref[:, 64:].astype(F32)
    channel = channel_ref[...].astype(F32)
    high = lax.Precision.HIGHEST
    small = dot(dot(channel, kept_cross, ((0,), (0,)), high), channel, ((1,), (0,)), high)
    small = jnp.concatenate([small, jnp.zeros((C, 128 - C), F32)], axis=1)
    small = jnp.concatenate([small, jnp.zeros((DEV - C, 128), F32)], axis=0)
    pack_chunks(coeff, stage, split_three(small), send_ref)
    for copy in kept:
        copy.wait()


def final_kernel(
    recv_ref, up_hbm, bypass_ref, channel_ref, same_ref, back_hbm,
    out_ref, up_ref, back_ref, stage, left, rows_ref, table_sem, up_sems, sems,
):
    (table_made,) = start_all((back_hbm, back_ref, table_sem))
    up_made = []
    for n in range(STEPS):
        some = pl.ds(PER * n, PER)
        up_made += start_all((up_hbm.at[some], up_ref.at[some], up_sems.at[n]))
    bypass_matrix(bypass_ref, channel_ref, same_ref, ((1,), (0,)), left)
    unpack_chunks(recv_ref, stage, left)
    made = copies(out_ref, rows_ref, sems, back=True)
    rows = rows_ref.reshape(TILES, ROWS, 128)
    table_made.wait()
    for n in range(STEPS):
        up_made[n].wait()
        for b in range(CX // XB):
            cells = block_of(up_ref, PER * n, b)
            right = jnp.concatenate([back_ref[:, WIDE * n : WIDE * (n + 1)], cells], axis=0)
            block_store(rows, PER * n, b, dot(left[b], right).astype(BF16))
        for copy in made[PER * n * GROUPS : PER * (n + 1) * GROUPS]:
            copy.start()
    for copy in made:
        copy.wait()


def turn(value, b, tiles):
    for s in range(Q3):
        for j in range(GROUPS):
            at = (s * GROUPS + j) * KY
            turned = value[at : at + KY].T
            for c in range(4):
                tiles[4 * j + c, s, b] = turned[32 * c : 32 * c + KX]


PAIR = 5


def outer_kernel(*refs):
    out_ref, first, second = refs[8:]

    @pl.when(pl.program_id(0) == 0)
    def _():
        for b in range(4):
            turn(unpack_modes(refs[b][...].astype(F32)), b, first)
            turn(unpack_modes(refs[4 + b][...].astype(F32)), b, second)

    c = pl.program_id(0) * PAIR
    for s in range(Q3):
        own = [[first[c + i, s, b] for b in range(4)] for i in range(PAIR)]
        for o in range(C):
            other = [second[o, s, b] for b in range(4)]
            for i in range(PAIR):
                terms = [own[i][b] * other[b] for b in range(4)]
                out_ref[i, o, s] = (terms[0] + terms[2]) + (terms[1] + terms[3])


def small_kernel(recv_ref, small_ref, stage):
    stage[...] = recv_ref[pl.ds(0, 24)].astype(F32)
    small_ref[...] = join_three(stage[:, CHUNK - 1, :])


def call(kernel, out, in_specs, scratch, limit=12, **more):
    return pl.pallas_call(
        kernel,
        out_shape=out,
        in_specs=in_specs,
        scratch_shapes=scratch,
        compiler_params=pltpu.CompilerParams(vmem_limit_bytes=limit * MIB),
        **more,
    )


def around(value):
    return [value] + [
        lax.ppermute(value, "dp", [(i, (i + k) % 4) for i in range(4)]) for k in (1, 2, 3)
    ]


def body(field, cotangent, spectral_weight, bypass_weight):
    table = {name: jnp.asarray(value) for name, value in TABLES.items()}
    shape = jax.ShapeDtypeStruct
    chunks = shape((DEV, CHUNK, 128), BF16)
    cells = shape((TILES, GROUPS, CX, 4, CY, 128), BF16)
    rows = shape((TILES, ROWS, 128), BF16)
    stage = pltpu.VMEM((DEV * CHUNK, 128), F32)
    dma = lambda *count: pltpu.SemaphoreType.DMA(count)
    sems = dma(TILES, GROUPS)
    field_t = jnp.transpose(field[0], (0, 2, 1, 3))
    cot_t = jnp.transpose(cotangent[0], (0, 2, 1, 3))
    weight_t = jnp.transpose(spectral_weight, (2, 3, 4, 0, 1))

    def exchange(value):
        return lax.all_to_all(value, ("gx", "gy"), 0, 0, tiled=True)

    send, field_rows = call(
        analyze_kernel, (chunks, cells), [HBM, HBM],
        [pltpu.VMEM(cells.shape, BF16), pltpu.VMEM((NP, 256), BF16),
         pltpu.VMEM((ROWS, 256), F32), stage, sems, dma(4), dma(4)],
        out_specs=(VMEM, HBM), limit=62,
    )(field_t, table["zt_ahead"])
    recv = exchange(send)
    weight = call(
        weights_kernel, shape((C, SPEC, 128), BF16), [VMEM], [], out_specs=VMEM,
    )(weight_t)
    send, own = call(
        mix_kernel, (chunks, shape((3 * PACK, 128), BF16)), [VMEM] * 4,
        [pltpu.VMEM((SPEC, 128), F32)], out_specs=(VMEM,) * 2, limit=12,
    )(recv, weight, table["x_ahead"], table["y_ahead"])
    recv = exchange(send)
    left = pltpu.VMEM((CX // XB, BLOCK, NQ + BLOCK), BF16)
    held = pltpu.VMEM(rows.shape, BF16)
    back = pltpu.VMEM((NQ, NP), BF16)
    send, up = call(
        point_kernel, (chunks, rows), [VMEM, HBM, HBM] + [VMEM] * 5,
        [held, pltpu.VMEM(cells.shape, BF16), held, stage, left, pltpu.VMEM((ROWS, 256), F32),
         pltpu.VMEM((BLOCK, BLOCK), F32), dma(2, STEPS), sems],
        out_specs=(VMEM, HBM), limit=51,
    )(recv, field_rows, cot_t, bypass_weight, table["channel"], table["same"],
      table["zt_back"], table["zt_ahead"])
    recv = exchange(send)
    specs = around(own)
    recv, *specs = lax.optimization_barrier((recv, *specs))
    send, spec_up = call(
        mix_back_kernel, (chunks, shape((3 * PACK, 128), BF16)), [VMEM] * 4, [stage],
        out_specs=(VMEM,) * 2,
    )(recv, weight, table["x_ahead"], table["y_ahead"])
    recv = exchange(send)
    specs += around(spec_up)
    grad_spectral = pl.pallas_call(
        outer_kernel,
        grid=(C // PAIR,),
        out_shape=shape((C, C, Q3, KX, KY), F32),
        in_specs=[VMEM] * 8,
        out_specs=pl.BlockSpec((PAIR, C, Q3, KX, KY), lambda c: (c, 0, 0, 0, 0)),
        scratch_shapes=[pltpu.VMEM((C, Q3, 4, KX, KY), F32)] * 2,
        compiler_params=pltpu.CompilerParams(vmem_limit_bytes=24 * MIB),
        cost_estimate=pl.CostEstimate(
            flops=10**9, bytes_accessed=10**8, transcendentals=0
        ),
    )(*specs)
    recv, grad_spectral = lax.optimization_barrier((recv, grad_spectral))
    small = call(
        small_kernel, shape((24, 128), F32), [VMEM], [pltpu.VMEM((24, CHUNK, 128), F32)],
        out_specs=VMEM,
    )(recv)
    smalls = around(small)
    grad_field = call(
        final_kernel, shape((CX, C, CY, NP), BF16), [VMEM, HBM, VMEM, VMEM, VMEM, HBM],
        [held, back, stage, left, pltpu.VMEM(cells.shape, BF16), pltpu.SemaphoreType.DMA,
         dma(STEPS), sems],
        out_specs=HBM, limit=60,
    )(recv, up, bypass_weight, table["channel"], table["same"], table["zt_back"])
    grad_bypass = ((smalls[0] + smalls[2]) + (smalls[1] + smalls[3]))[:C, :C]
    return (
        jnp.transpose(grad_field, (0, 2, 1, 3))[None],
        jnp.transpose(grad_spectral, (3, 4, 0, 1, 2)),
        grad_bypass,
    )


def solution(mesh):
    in_specs = (
        P("dp", "gx", "gy", None, None),
        P("dp", "gx", "gy", None, None),
        P(None, None, None, None, ("gx", "gy")),
        P(),
    )
    out_specs = (P("dp", "gx", "gy", None, None), P(None, None, None, None, ("gx", "gy")), P())
    return jax.shard_map(body, mesh=mesh, in_specs=in_specs, out_specs=out_specs, check_vma=False)
```
